32 devices in a mesh: gx: 2 (over y), gy: 4 (over z), ba: 4 (over x, core).
Axes of the slice: x: 2, y: 2, z: 4, core: 2. Of those that a mesh axis runs over, the one named last changes fastest.
Arguments:
- moved_fields: float32 [2, 4, 4, 4, 4, 4096], P('gx', 'gy', 'ba'), may hold values from -0.1 to 1.4, as said below
- send_slot: int32 [2, 4, 4, 4, 1], P('gx', 'gy', 'ba'), may hold values from -1 to 3, as said below
- recv_index: int32 [2, 4, 4, 2], P('gx', 'gy', 'ba'), may hold values from 0 to 3, as said below
- site_kind: int32 [32, 64, 128], P('gx', 'gy', 'ba'), may hold values from 0 to 3
Outputs:
- distributions: float32 [19, 32, 64, 128], P(None, 'gx', 'gy', 'ba')
The draws below stay inside these ranges and needn't reach their ends.
Inputs may be any that keep to these rules, and one draw needn't show every extreme that they name: Blocks move only between devices with the same gx and ba. Within such a group, the live entries of one device's send_slot are distinct slots; the entry [p, c] is live exactly when some device p' = p of the group has recv_index p_sender + c naming this device, and every device receives exactly 2 blocks, each from one live entry. A device sends at most 1 block to one peer; the number of live slots of a device varies. `recv_index`: entries are distinct within a device and consistent with send_slot as stated there. `moved_fields`: component 0 is the density, between 0.6 and 1.4; components 1 to 3 are velocities between -0.1 and 0.1; slots that no live send_slot entry names hold values of the same kind.
All inputs are finite; a program needn't handle non-finite values.
Results may differ from the reference program's by a relative error of at most 0.0003.
Values sent between devices are 32-bit elements; how exact they have to be, the bound alone decides.
A program may use at most 64 MiB of HBM per device.

```python
import jax
import jax.numpy as jnp

BLOCK = 16
B_DEV = 2
STEPS = 4
CAP = 1
SLOTS = 4
NX = 32
NY = 64
NZ = 128
N_GX = 2
N_GY = 4
N_BA = 4


def route_group(group_key):
    bias_key, pick_key, slot_key = jax.random.split(group_key, 3)
    sources = jnp.arange(N_GY, dtype=jnp.int32)
    source_bias = jax.random.randint(bias_key, (N_GY,), 0, 4)
    pick_noise = jax.random.randint(pick_key, (N_GY, N_GY), 0, 1024)
    scores = (pick_noise + 1024 * source_bias[None, :]) * N_GY + sources[None, :]
    ranked_sources = jnp.argsort(-scores, axis=1).astype(jnp.int32)
    position = jnp.argsort(ranked_sources, axis=1).astype(jnp.int32)
    block_ids = jnp.arange(B_DEV, dtype=jnp.int32)
    receives = ranked_sources[:, block_ids % N_GY] * CAP + block_ids // N_GY
    rank_ids = jnp.arange(CAP, dtype=jnp.int32)
    is_live = position.T[:, :, None] + N_GY * rank_ids[None, None, :] < B_DEV
    live_flat = is_live.reshape(N_GY, N_GY * CAP)
    slot_noise = jax.random.randint(slot_key, (N_GY, N_GY * CAP), 0, 1048576) * (N_GY * CAP) + jnp.arange(N_GY * CAP, dtype=jnp.int32)[None, :]
    higher = (slot_noise[:, None, :] > slot_noise[:, :, None]) & live_flat[:, None, :]
    rank_live = jnp.sum(higher.astype(jnp.int32), axis=2)
    send_table = jnp.where(live_flat, SLOTS - 1 - rank_live, -1).reshape(N_GY, N_GY, CAP)
    return (send_table.astype(jnp.int32), receives.astype(jnp.int32))


def routes(base_key):
    group_keys = jax.random.split(jax.random.fold_in(base_key, 11), N_GX * N_BA)
    send_table, receives = jax.vmap(route_group)(group_keys)
    send_table = send_table.reshape(N_GX, N_BA, N_GY, N_GY, CAP).transpose(0, 2, 1, 3, 4)
    receives = receives.reshape(N_GX, N_BA, N_GY, B_DEV).transpose(0, 2, 1, 3)
    return (send_table, receives)


def draw_send_slot(key, part):
    return routes(key)[0]


def draw_recv_index(key, part):
    return routes(key)[1]


def draw_moved_fields(key, part):
    shape = (N_GX, N_GY, N_BA, SLOTS, BLOCK ** 3)
    density_key, speed_key = jax.random.split(jax.random.fold_in(key, 3))
    density = jax.random.uniform(density_key, shape, dtype=jnp.float32, minval=0.6, maxval=1.4)
    speeds = jax.random.uniform(speed_key, (3,) + shape, dtype=jnp.float32, minval=-0.1, maxval=0.1)
    stacked = jnp.concatenate([density[None], speeds], axis=0)
    return stacked.transpose(1, 2, 3, 4, 0, 5)


def draw_site_kind(key, part):
    base_key = jax.random.fold_in(key, 5)
    radius_key, center_key, present_key = jax.random.split(base_key, 3)
    columns_x = NX // BLOCK
    columns_y = NY // BLOCK
    top_radius = max(BLOCK // 2, 2)
    radius = jax.random.randint(radius_key, (columns_x, columns_y), 1, top_radius + 1)
    center_pick = jax.random.randint(center_key, (2, columns_x, columns_y), 0, 1048576)
    span = jnp.maximum(BLOCK - 2 * radius + 1, 1)
    center_x = radius + center_pick[0] % span
    center_y = radius + center_pick[1] % span
    present = jax.random.randint(present_key, (columns_x, columns_y), 0, 4) > 0
    site_x = jnp.arange(NX, dtype=jnp.int32)
    site_y = jnp.arange(NY, dtype=jnp.int32)
    column_x = site_x // BLOCK
    column_y = site_y // BLOCK
    local_x = site_x % BLOCK
    local_y = site_y % BLOCK
    radius_here = radius[column_x][:, column_y]
    cx_here = center_x[column_x][:, column_y]
    cy_here = center_y[column_x][:, column_y]
    present_here = present[column_x][:, column_y]
    offset_x = local_x[:, None] - cx_here
    offset_y = local_y[None, :] - cy_here
    distance = offset_x * offset_x + offset_y * offset_y
    inside = (distance < radius_here * radius_here) & present_here
    site_z = jnp.arange(NZ, dtype=jnp.int32)[None, None, :]
    inside3 = inside[:, :, None]
    kinds = jnp.where(inside3, jnp.where(site_z == 0, 2, jnp.where(site_z == NZ - 1, 3, 0)), 1)
    return kinds.astype(jnp.int32)


def setup_inputs(seed: int = 0) -> dict:
    seeds = jax.random.split(jax.random.key(seed), 5)
    moved_fields = draw_moved_fields(jax.random.fold_in(seeds[4], 71), 0)
    send_slot = draw_send_slot(jax.random.fold_in(seeds[4], 71), 0)
    recv_index = draw_recv_index(jax.random.fold_in(seeds[4], 71), 0)
    site_kind = draw_site_kind(jax.random.fold_in(seeds[4], 71), 0)
    return {"moved_fields": moved_fields, "send_slot": send_slot, "recv_index": recv_index, "site_kind": site_kind}


VELOCITIES = ((0, 0, 0), (1, 0, 0), (-1, 0, 0), (0, 1, 0), (0, -1, 0), (0, 0, 1), (0, 0, -1),
              (1, 1, 0), (-1, -1, 0), (1, -1, 0), (-1, 1, 0), (1, 0, 1), (-1, 0, -1),
              (1, 0, -1), (-1, 0, 1), (0, 1, 1), (0, -1, -1), (0, 1, -1), (0, -1, 1))
WEIGHTS = (1.0 / 3.0,) + (1.0 / 18.0,) * 6 + (1.0 / 36.0,) * 12
OPPOSITE = (0, 2, 1, 4, 3, 6, 5, 8, 7, 10, 9, 12, 11, 14, 13, 16, 15, 18, 17)
RELAX_RATE = 1.25
INLET_SPEED = 0.05


def dotted(vector, speeds):
    running = None
    for sign_value, component in zip(vector, speeds):
        if sign_value != 0:
            signed_term = component if sign_value > 0 else -component
            running = signed_term if running is None else running + signed_term
    return running


def equilibrium_one(direction_id, density, speeds, squared):
    baseline = 1.0 - 1.5 * squared
    projected = dotted(VELOCITIES[direction_id], speeds)
    if projected is None:
        return WEIGHTS[direction_id] * density * baseline
    return WEIGHTS[direction_id] * density * (baseline + 3.0 * projected + 4.5 * projected * projected)


def square_of(speeds):
    return speeds[0] * speeds[0] + speeds[1] * speeds[1] + speeds[2] * speeds[2]


def collide(populations, site_kind):
    density = populations[0]
    for member in populations[1:]:
        density = density + member
    speeds = []
    for axis_id in range(3):
        momentum = None
        for vector, member in zip(VELOCITIES, populations):
            if vector[axis_id] != 0:
                signed_term = member if vector[axis_id] > 0 else -member
                momentum = signed_term if momentum is None else momentum + signed_term
        speeds.append(momentum / density)
    squared = square_of(speeds)
    inlet_speeds = (0.0, 0.0, INLET_SPEED)
    inlet_squared = square_of(inlet_speeds)
    result = []
    for direction_id in range(19):
        balanced = equilibrium_one(direction_id, density, speeds, squared)
        outflow = equilibrium_one(direction_id, 1.0, speeds, squared)
        inflow = equilibrium_one(direction_id, 1.0, inlet_speeds, inlet_squared)
        relaxed = populations[direction_id] + RELAX_RATE * (balanced - populations[direction_id])
        updated = jnp.where(site_kind == 3, outflow, relaxed)
        updated = jnp.where(site_kind == 2, inflow, updated)
        updated = jnp.where(site_kind == 1, populations[OPPOSITE[direction_id]], updated)
        result.append(updated)
    return result


def initial_populations(fields):
    speeds = (fields[1], fields[2], fields[3])
    squared = square_of(speeds)
    return [equilibrium_one(direction_id, fields[0], speeds, squared) for direction_id in range(19)]


def rebalance(moved_fields, send_slot, recv_index):
    gx_ids = jnp.arange(N_GX, dtype=jnp.int32)[:, None, None, None]
    gy_ids = jnp.arange(N_GY, dtype=jnp.int32)[None, :, None, None]
    ba_ids = jnp.arange(N_BA, dtype=jnp.int32)[None, None, :, None]
    senders = (recv_index // CAP).astype(jnp.int32)
    sender_rank = (recv_index % CAP).astype(jnp.int32)
    slot_ids = send_slot[gx_ids, senders, ba_ids, gy_ids, sender_rank]
    blocks = moved_fields[gx_ids, senders, ba_ids, slot_ids]
    blocks = blocks.reshape(N_GX, N_GY, N_BA, B_DEV, 4, BLOCK, BLOCK, BLOCK)
    blocks = blocks.transpose(4, 0, 5, 1, 6, 2, 3, 7)
    return blocks.reshape(4, N_GX * BLOCK, N_GY * BLOCK, N_BA * B_DEV * BLOCK)


def reference(moved_fields, send_slot, recv_index, site_kind):
    fields = rebalance(moved_fields, send_slot, recv_index)
    populations = initial_populations(fields)
    for step_id in range(STEPS):
        collided = collide(populations, site_kind)
        populations = [jnp.roll(member, vector, axis=(0, 1, 2)) for member, vector in zip(collided, VELOCITIES)]
    return jnp.stack(populations)
```

```python
import functools

import jax
import jax.numpy as jnp
from jax import lax
from jax.experimental import pallas as pl
from jax.experimental.pallas import tpu as pltpu
from jax.sharding import PartitionSpec as P

STEPS = 4
HALO = STEPS
PAIRS = (
    (1, 0, 0),
    (0, 1, 0),
    (0, 0, 1),
    (1, 1, 0),
    (1, -1, 0),
    (1, 0, 1),
    (1, 0, -1),
    (0, 1, 1),
    (0, 1, -1),
)
VELOCITIES = ((0, 0, 0),) + tuple(
    tuple(sign * part for part in vector) for vector in PAIRS for sign in (1, -1)
)
WEIGHTS = (1.0 / 3.0,) + (1.0 / 18.0,) * 6 + (1.0 / 36.0,) * 12
RELAX_RATE = 1.25
INLET_SPEED = 0.05
SUBLANES = 8
LANES = 128


def padded_2(array, sides, width):
    for axis, dim in sides:
        devices, length = (lax.axis_size(axis), array.shape[dim])
        up = [(i, (i + 1) % devices) for i in range(devices)]
        down = [(j, i) for i, j in up]
        last = lax.slice_in_dim(array, length - width, length, axis=dim)
        initial = lax.slice_in_dim(array, 0, width, axis=dim)
        before = lax.ppermute(last, axis, up)
        after = lax.ppermute(initial, axis, down)
        array = jnp.concatenate([before, array, after], axis=dim)
    return array


def dotted(vector, speeds):
    running = None
    for sign_value, component in zip(vector, speeds):
        if sign_value > 0:
            running = component if running is None else running + component
        elif sign_value < 0:
            running = -component if running is None else running - component
    return running


def row_ids():
    return lax.broadcasted_iota(jnp.int32, (SUBLANES, LANES), 0)


def shifted(plane, rows, stride, step_y, step_z):
    if step_y:
        rolled = pltpu.roll(plane, step_y % SUBLANES, 0)
        crossed = pltpu.roll(rolled, (step_y * stride) % LANES, 1)
        plane = jnp.where(rows == (0 if step_y > 0 else SUBLANES - 1), crossed, rolled)
    if step_z:
        plane = pltpu.roll(plane, step_z % LANES, 1)
    return plane


def squared_base(speeds):
    return 1.0 - (1.0 / 6.0) * (
        speeds[0] * speeds[0] + speeds[1] * speeds[1] + speeds[2] * speeds[2]
    )


def start_plane(fields, kind):
    wall, inlet = kind == 1.0, kind == 2.0
    factor = jnp.where(kind <= 1.0, fields[0], 1.0)
    scale = jnp.where(wall, -3.0, jnp.where(inlet, 0.0, 3.0))
    speeds = [scale * fields[axis] for axis in (1, 2, 3)]
    speeds[2] = jnp.where(inlet, 3.0 * INLET_SPEED, speeds[2])
    base = squared_base(speeds)
    result = [WEIGHTS[0] * factor * base]
    weighted = {w: w * factor for w in set(WEIGHTS[1:])}
    for pair_id, vector in enumerate(PAIRS):
        w = weighted[WEIGHTS[1 + 2 * pair_id]]
        projected = dotted(vector, speeds)
        even = w * (base + 0.5 * projected * projected)
        odd = w * projected
        result += [even + odd, even - odd]
    return result


def collide_plane(populations, kind):
    fluid, wall, inlet = kind == 0.0, kind == 1.0, kind == 2.0
    sums = [populations[i] + populations[i + 1] for i in range(1, 19, 2)]
    differences = [populations[i] - populations[i + 1] for i in range(1, 19, 2)]
    density = populations[0]
    for member in sums:
        density = density + member
    triple = 3.0 / density
    speeds = []
    for axis in range(3):
        momentum = dotted([vector[axis] for vector in PAIRS], differences)
        speeds.append(jnp.where(wall | inlet, 0.0, momentum * triple))
    speeds[2] = jnp.where(inlet, 3.0 * INLET_SPEED, speeds[2])
    base = squared_base(speeds)
    factor = jnp.where(fluid, RELAX_RATE * density, jnp.where(wall, 0.0, 1.0))
    keep = jnp.where(fluid, 1.0 - RELAX_RATE, jnp.where(wall, 1.0, 0.0))
    half_even = 0.5 * keep
    half_odd = jnp.where(wall, -0.5, half_even)
    result = [keep * populations[0] + WEIGHTS[0] * factor * base]
    weighted = {w: w * factor for w in set(WEIGHTS[1:])}
    for pair_id, vector in enumerate(PAIRS):
        w = weighted[WEIGHTS[1 + 2 * pair_id]]
        projected = dotted(vector, speeds)
        even = half_even * sums[pair_id] + w * (base + 0.5 * projected * projected)
        odd = half_odd * differences[pair_id] + w * projected
        result += [even + odd, even - odd]
    return result


def lattice_kernel(fields_ref, out_ref, first, second):
    planes = fields_ref.shape[1]
    extent_y, extent_z = out_ref.shape[2:]
    stride = extent_z + 2 * HALO
    rows = row_ids()

    def begin(x, carry):
        fields = [fields_ref[i, x] for i in range(5)]
        for i, member in enumerate(start_plane(fields, fields[4])):
            first[i, x] = member
        return carry

    lax.fori_loop(0, planes, begin, 0)
    source, target = first, second
    for step in range(1, STEPS):

        def advance(x, carry, source=source, target=target):
            pulled = [
                shifted(source[i, x - v[0]], rows, stride, v[1], v[2])
                for i, v in enumerate(VELOCITIES)
            ]
            for i, member in enumerate(collide_plane(pulled, fields_ref[4, x])):
                target[i, x] = member
            return carry

        lax.fori_loop(step, planes - step, advance, 0)
        source, target = target, source

    def finish(x, carry):
        for i, v in enumerate(VELOCITIES):
            plane = source[i, x + HALO - v[0]]
            offset = HALO - v[1]
            plane = pltpu.roll(plane, SUBLANES - offset, 0)
            crossed = pltpu.roll(plane, LANES - stride, 1)
            plane = jnp.where(rows < SUBLANES - offset, plane, crossed)
            for group in range(extent_y // SUBLANES):
                part = pltpu.roll(plane, LANES - (group * stride + HALO - v[2]), 1)
                out_ref[i, x, pl.ds(group * SUBLANES, SUBLANES), :] = part[:, :extent_z]
        return carry

    lax.fori_loop(0, out_ref.shape[1], finish, 0)


def lattice(fields, extents):
    planes = fields.shape[1]
    return pl.pallas_call(
        lattice_kernel,
        out_shape=jax.ShapeDtypeStruct((19,) + tuple(extents), jnp.float32),
        in_specs=[pl.BlockSpec(memory_space=pltpu.VMEM)],
        out_specs=pl.BlockSpec(memory_space=pltpu.VMEM),
        scratch_shapes=[pltpu.VMEM((19, planes, SUBLANES, LANES), jnp.float32)] * 2,
        compiler_params=pltpu.CompilerParams(vmem_limit_bytes=24 * 1024 * 1024),
        name="lattice",
    )(fields)


def on_device(moved_fields, send_slot, recv_index, site_kind):
    held_blocks = moved_fields[0, 0, 0]
    wanted = send_slot[0, 0, 0]
    peer_count = wanted.shape[0]
    per_peer = wanted.shape[1]
    flat_wanted = wanted.reshape(peer_count * per_peer)
    picked = jnp.take(held_blocks, jnp.maximum(flat_wanted, 0), axis=0)
    picked = jnp.where((flat_wanted >= 0)[:, None, None], picked, 0.0)
    outgoing = picked.reshape(peer_count, per_peer, held_blocks.shape[1], held_blocks.shape[2])
    arrived = lax.all_to_all(outgoing, "gy", split_axis=0, concat_axis=0, tiled=True)
    arrived = arrived.reshape(peer_count * per_peer, held_blocks.shape[1], held_blocks.shape[2])
    placed = jnp.take(arrived, recv_index[0, 0, 0], axis=0)
    block_edge = site_kind.shape[0]
    blocks_here = placed.shape[0]
    placed = placed.reshape(blocks_here, 4, block_edge, block_edge, block_edge)
    placed = placed.transpose(1, 2, 3, 0, 4).reshape(
        4, block_edge, block_edge, blocks_here * block_edge
    )
    fields = jnp.concatenate([placed, site_kind[None].astype(jnp.float32)])
    fields = padded_2(fields, (("gx", 1), ("gy", 2), ("ba", 3)), HALO)
    parts, extent_x, extent_y, extent_z = fields.shape
    groups = extent_y // SUBLANES
    packed = fields.reshape(parts, extent_x, groups, SUBLANES, extent_z)
    packed = packed.transpose(0, 1, 3, 2, 4).reshape(parts, extent_x, SUBLANES, -1)
    packed = jnp.pad(packed, ((0, 0), (0, 0), (0, 0), (0, LANES - packed.shape[3])))
    return lattice(packed, site_kind.shape)


def solution(mesh):
    return jax.shard_map(
        on_device,
        mesh=mesh,
        in_specs=(
            P("gx", "gy", "ba", None, None, None),
            P("gx", "gy", "ba", None, None),
            P("gx", "gy", "ba", None),
            P("gx", "gy", "ba"),
        ),
        out_specs=P(None, "gx", "gy", "ba"),
        check_vma=False,
    )
```

```python
import functools

import jax
import jax.numpy as jnp
from jax import lax
from jax.experimental import pallas as pl
from jax.experimental.pallas import tpu as pltpu
from jax.sharding import PartitionSpec as P

STEPS = 4
HALO = STEPS
PAIRS = (
    (1, 0, 0),
    (0, 1, 0),
    (0, 0, 1),
    (1, 1, 0),
    (1, -1, 0),
    (1, 0, 1),
    (1, 0, -1),
    (0, 1, 1),
    (0, 1, -1),
)
VELOCITIES = ((0, 0, 0),) + tuple(
    tuple(sign * part for part in vector) for vector in PAIRS for sign in (1, -1)
)
WEIGHTS = (1.0 / 3.0,) + (1.0 / 18.0,) * 6 + (1.0 / 36.0,) * 12
RELAX_RATE = 1.25
INLET_SPEED = 0.05
SUBLANES = 8
LANES = 128


def dotted(vector, speeds):
    running = None
    for sign_value, component in zip(vector, speeds):
        if sign_value > 0:
            running = component if running is None else running + component
        elif sign_value < 0:
            running = -component if running is None else running - component
    return running


def row_ids():
    return lax.broadcasted_iota(jnp.int32, (SUBLANES, LANES), 0)


def shifted(plane, rows, stride, step_y, step_z):
    if step_y:
        rolled = pltpu.roll(plane, step_y % SUBLANES, 0)
        crossed = pltpu.roll(rolled, (step_y * stride) % LANES, 1)
        plane = jnp.where(rows == (0 if step_y > 0 else SUBLANES - 1), crossed, rolled)
    if step_z:
        plane = pltpu.roll(plane, step_z % LANES, 1)
    return plane


def squared_base(speeds):
    return 1.0 - (1.0 / 6.0) * (
        speeds[0] * speeds[0] + speeds[1] * speeds[1] + speeds[2] * speeds[2]
    )


def start_plane(fields, kind):
    wall, inlet = kind == 1.0, kind == 2.0
    factor = jnp.where(kind <= 1.0, fields[0], 1.0)
    scale = jnp.where(wall, -3.0, jnp.where(inlet, 0.0, 3.0))
    speeds = [scale * fields[axis] for axis in (1, 2, 3)]
    speeds[2] = jnp.where(inlet, 3.0 * INLET_SPEED, speeds[2])
    base = squared_base(speeds)
    result = [WEIGHTS[0] * factor * base]
    weighted = {w: w * factor for w in set(WEIGHTS[1:])}
    for pair_id, vector in enumerate(PAIRS):
        w = weighted[WEIGHTS[1 + 2 * pair_id]]
        projected = dotted(vector, speeds)
        even = w * (base + 0.5 * projected * projected)
        odd = w * projected
        result += [even + odd, even - odd]
    return result


def collide_plane(populations, kind):
    fluid, wall, inlet = kind == 0.0, kind == 1.0, kind == 2.0
    sums = [populations[i] + populations[i + 1] for i in range(1, 19, 2)]
    differences = [populations[i] - populations[i + 1] for i in range(1, 19, 2)]
    density = populations[0]
    for member in sums:
        density = density + member
    triple = 3.0 / density
    speeds = []
    for axis in range(3):
        momentum = dotted([vector[axis] for vector in PAIRS], differences)
        speeds.append(jnp.where(wall | inlet, 0.0, momentum * triple))
    speeds[2] = jnp.where(inlet, 3.0 * INLET_SPEED, speeds[2])
    base = squared_base(speeds)
    factor = jnp.where(fluid, RELAX_RATE * density, jnp.where(wall, 0.0, 1.0))
    keep = jnp.where(fluid, 1.0 - RELAX_RATE, jnp.where(wall, 1.0, 0.0))
    half_even = 0.5 * keep
    half_odd = jnp.where(wall, -0.5, half_even)
    result = [keep * populations[0] + WEIGHTS[0] * factor * base]
    weighted = {w: w * factor for w in set(WEIGHTS[1:])}
    for pair_id, vector in enumerate(PAIRS):
        w = weighted[WEIGHTS[1 + 2 * pair_id]]
        projected = dotted(vector, speeds)
        even = half_even * sums[pair_id] + w * (base + 0.5 * projected * projected)
        odd = half_odd * differences[pair_id] + w * projected
        result += [even + odd, even - odd]
    return result


def lattice_kernel(fields_ref, out_ref, first, second):
    planes = fields_ref.shape[1]
    extent_y, extent_z = out_ref.shape[2:]
    stride = extent_z + 2 * HALO
    rows = row_ids()

    def begin(x, carry):
        fields = [fields_ref[i, x] for i in range(5)]
        for i, member in enumerate(start_plane(fields, fields[4])):
            first[i, x] = member
        return carry

    lax.fori_loop(0, planes, begin, 0)
    source, target = first, second
    for step in range(1, STEPS):

        def advance(x, carry, source=source, target=target):
            pulled = [
                shifted(source[i, x - v[0]], rows, stride, v[1], v[2])
                for i, v in enumerate(VELOCITIES)
            ]
            for i, member in enumerate(collide_plane(pulled, fields_ref[4, x])):
                target[i, x] = member
            return carry

        lax.fori_loop(step, planes - step, advance, 0)
        source, target = target, source

    def finish(x, carry):
        for i, v in enumerate(VELOCITIES):
            plane = source[i, x + HALO - v[0]]
            offset = HALO - v[1]
            plane = pltpu.roll(plane, SUBLANES - offset, 0)
            crossed = pltpu.roll(plane, LANES - stride, 1)
            plane = jnp.where(rows < SUBLANES - offset, plane, crossed)
            for group in range(extent_y // SUBLANES):
                part = pltpu.roll(plane, LANES - (group * stride + HALO - v[2]), 1)
                out_ref[i, x, pl.ds(group * SUBLANES, SUBLANES), :] = part[:, :extent_z]
        return carry

    lax.fori_loop(0, out_ref.shape[1], finish, 0)


def lattice(fields, extents):
    planes = fields.shape[1]
    return pl.pallas_call(
        lattice_kernel,
        out_shape=jax.ShapeDtypeStruct((19,) + tuple(extents), jnp.float32),
        in_specs=[pl.BlockSpec(memory_space=pltpu.VMEM)],
        out_specs=pl.BlockSpec(memory_space=pltpu.VMEM),
        scratch_shapes=[pltpu.VMEM((19, planes, SUBLANES, LANES), jnp.float32)] * 2,
        compiler_params=pltpu.CompilerParams(vmem_limit_bytes=24 * 1024 * 1024),
        name="lattice",
    )(fields)


def mesh_device(**moved):
    return tuple(moved.get(axis, lax.axis_index(axis)) for axis in ("gx", "gy", "ba"))


def remote(source, target, send_sem, recv_sem, device):
    return pltpu.make_async_remote_copy(
        src_ref=source,
        dst_ref=target,
        send_sem=send_sem,
        recv_sem=recv_sem,
        device_id=device,
        device_id_type=pl.DeviceIdType.MESH,
    )


def grouped(low, high, rows, lanes, stride):
    middle = pltpu.roll(jnp.where(rows < HALO, low, high), stride, 1)
    last = pltpu.roll(high, 2 * stride, 1)
    return jnp.where(lanes < stride, low, jnp.where(lanes < 2 * stride, middle, last))


def gather_kernel(
    moved_ref,
    slot_ref,
    index_ref,
    kind_ref,
    out_ref,
    staged,
    arrived,
    chosen,
    side_x,
    kind_wide,
    kind_x,
    send_y,
    side_y,
    send_z,
    side_z,
    sent_sem,
    arrived_sem,
    halo_sent,
    halo_arrived,
):
    extent_x, extent_y, extent_z = kind_ref.shape
    blocks = chosen.shape[0]
    edge = extent_z // blocks
    stride = extent_z + 2 * HALO
    planes = extent_x + 2 * HALO
    rows = row_ids()
    lanes = lax.broadcasted_iota(jnp.int32, (SUBLANES, LANES), 1)
    me = {axis: lax.axis_index(axis) for axis in ("gx", "gy", "ba")}
    size = {axis: lax.axis_size(axis) for axis in ("gx", "gy", "ba")}
    up = {a: mesh_device(**{a: lax.rem(me[a] + 1, size[a])}) for a in me}
    down = {a: mesh_device(**{a: lax.rem(me[a] + size[a] - 1, size[a])}) for a in me}
    peers = [lax.rem(me["gy"] + offset, size["gy"]) for offset in range(size["gy"])]

    barrier = pltpu.get_barrier_semaphore()
    greeted = [mesh_device(gy=peer) for peer in peers[1:]]
    greeted += [up["gx"], down["gx"], up["ba"], down["ba"]]
    for device in greeted:
        pl.semaphore_signal(
            barrier, inc=1, device_id=device, device_id_type=pl.DeviceIdType.MESH
        )
    for offset in range(1, size["gy"]):
        staged[offset] = moved_ref[jnp.maximum(slot_ref[peers[offset]], 0)]
    pl.semaphore_wait(barrier, len(greeted))

    moves = []
    for offset in range(1, size["gy"]):
        moves.append(
            remote(
                staged.at[offset],
                arrived.at[me["gy"]],
                sent_sem.at[offset],
                arrived_sem.at[offset],
                mesh_device(gy=peers[offset]),
            )
        )
        moves[-1].start()
    arrived[me["gy"]] = moved_ref[jnp.maximum(slot_ref[me["gy"]], 0)]

    def halo(axis, number, low_source, high_source, target):
        pair = [
            remote(
                high_source,
                target.at[0],
                halo_sent.at[2 * number],
                halo_arrived.at[2 * number],
                up[axis],
            ),
            remote(
                low_source,
                target.at[1],
                halo_sent.at[2 * number + 1],
                halo_arrived.at[2 * number + 1],
                down[axis],
            ),
        ]
        for copy in pair:
            copy.start()
        return pair

    def lay_kind(x, carry):
        parts = []
        for half in range(2):
            kind_wide[x, half, :, pl.ds(0, extent_z)] = kind_ref[
                x, pl.ds(half * SUBLANES, SUBLANES), :
            ].astype(jnp.float32)
            wide = pltpu.roll(kind_wide[x, half], HALO, 0)
            parts.append(pltpu.roll(wide, HALO, 1))
        out_ref[4, x + HALO] = grouped(parts[0], parts[1], rows, lanes, stride)
        return carry

    lax.fori_loop(0, extent_x, lay_kind, 0)
    kind_copies = halo(
        "gx",
        0,
        out_ref.at[4, pl.ds(HALO, HALO)],
        out_ref.at[4, pl.ds(extent_x, HALO)],
        kind_x,
    )

    for move in moves:
        move.wait_recv()
    for block in range(blocks):
        chosen[block] = arrived[index_ref[block]]

    plane_size = edge * edge
    layers = HALO * plane_size
    x_copies = halo(
        "gx",
        1,
        chosen.at[:, :, pl.ds(0, layers)],
        chosen.at[:, :, pl.ds(extent_x * plane_size - layers, layers)],
        side_x,
    )

    def lay_fields(read, x, target_x):
        tiles = []
        for block in range(2):
            for half in range(2):
                start = pl.multiple_of(x * plane_size + half * LANES, LANES)
                tiles.append(read(block, pl.ds(start, LANES)))
        quarter, half_lanes, whole = LANES // 4, LANES // 2, LANES
        for part in range(4):
            picked = []
            for source, tile in enumerate(tiles):
                row = jnp.broadcast_to(tile[part : part + 1], (SUBLANES, LANES))
                turned = pltpu.roll(row, half_lanes, 1)
                low_first = (rows >= HALO) == (source % 2 == 0)
                picked.append(jnp.where(low_first, row, turned))
            pairs = []
            for block in range(2):
                pair = jnp.where(lanes < half_lanes, picked[2 * block], picked[2 * block + 1])
                shift = quarter if block else whole - quarter
                turned = pltpu.roll(pair, shift, 1)
                stays = ((rows & 2) == 0) == (block == 0)
                pairs.append(jnp.where(stays, pair, turned))
            joined = jnp.where((lanes & quarter) == 0, pairs[0], pairs[1])
            joined = jnp.where((rows & 1) == 0, joined, pltpu.roll(joined, whole - edge, 1))
            near = pltpu.roll(joined, HALO, 1)
            far = pltpu.roll(joined, (HALO + edge - quarter) % whole, 1)
            low = jnp.where((lanes & (half_lanes - 1)) < HALO + edge, near, far)
            high = pltpu.roll(low, half_lanes, 1)
            out_ref[part, target_x] = grouped(low, high, rows, lanes, stride)

    def lay_own(x, carry):
        lay_fields(lambda block, cut: chosen[block, :, cut], x, x + HALO)
        return carry

    lax.fori_loop(0, extent_x, lay_own, 0)
    for copy in kind_copies:
        copy.wait()
    for copy in x_copies:
        copy.wait_recv()

    for side in range(2):
        first_x = side * (extent_x + HALO)

        def lay_side(x, carry, side=side, first_x=first_x):
            lay_fields(lambda block, cut: side_x[side, block, :, cut], x, first_x + x)
            out_ref[4, first_x + x] = kind_x[side, x]
            return carry

        lax.fori_loop(0, HALO, lay_side, 0)

    per_y = 6
    count_y = planes // per_y

    def pack_y(index, carry):
        part, first_x = index // count_y, (index % count_y) * per_y
        own = [out_ref[part, first_x + k] for k in range(per_y)]
        for side in range(2):
            merged = []
            for half in range(2):
                total = None
                for group in range(3):
                    shift = (group * stride - (0 if side == 0 else 2 * stride)) % LANES
                    piece = own[half * 3 + group]
                    piece = pltpu.roll(piece, shift, 1) if shift else piece
                    total = piece if group == 0 else jnp.where(lanes < group * stride, total, piece)
                merged.append(total)
            other = pltpu.roll(merged[1], HALO, 0)
            keep = rows >= HALO if side == 0 else rows < HALO
            send_y[side, index] = jnp.where(keep, merged[0], other)
        return carry

    lax.fori_loop(0, 5 * count_y, pack_y, 0)
    y_copies = halo("gy", 2, send_y.at[0], send_y.at[1], side_y)
    for copy in y_copies:
        copy.wait_recv()

    def unpack_y(index, carry):
        part, first_x = index // count_y, (index % count_y) * per_y
        near = [side_y[0, index], pltpu.roll(side_y[0, index], HALO, 0)]
        far = [side_y[1, index], pltpu.roll(side_y[1, index], HALO, 0)]
        for half in range(2):
            for group in range(3):
                x = first_x + half * 3 + group
                back = (-group * stride) % LANES
                ahead = ((2 - group) * stride) % LANES
                near_piece = pltpu.roll(near[half], back, 1) if back else near[half]
                far_piece = pltpu.roll(far[half], ahead, 1) if ahead else far[half]
                plane = out_ref[part, x]
                plane = jnp.where((rows < HALO) & (lanes < stride), near_piece, plane)
                plane = jnp.where((rows >= HALO) & (lanes >= 2 * stride), far_piece, plane)
                out_ref[part, x] = plane
        return carry

    lax.fori_loop(0, 5 * count_y, unpack_y, 0)

    per_z = 8
    count_z = planes // per_z
    column = lax.rem(lanes, stride)

    def pack_z(index, carry):
        part, first_x = index // count_z, (index % count_z) * per_z
        own = [out_ref[part, first_x + k] for k in range(per_z)]
        for side in range(2):
            begin = HALO if side == 0 else extent_z
            total = None
            for k in range(per_z):
                shift = (k * HALO - begin) % LANES
                piece = pltpu.roll(own[k], shift, 1) if shift else own[k]
                total = piece if k == 0 else jnp.where(column < k * HALO, total, piece)
            send_z[side, index] = total
        return carry

    lax.fori_loop(0, 5 * count_z, pack_z, 0)
    z_copies = halo("ba", 3, send_z.at[0], send_z.at[1], side_z)
    for copy in z_copies:
        copy.wait_recv()

    def unpack_z(index, carry):
        part, first_x = index // count_z, (index % count_z) * per_z
        near, far = side_z[0, index], side_z[1, index]
        for k in range(per_z):
            back = (-k * HALO) % LANES
            ahead = (HALO + extent_z - k * HALO) % LANES
            near_piece = pltpu.roll(near, back, 1) if back else near
            far_piece = pltpu.roll(far, ahead, 1) if ahead else far
            plane = out_ref[part, first_x + k]
            plane = jnp.where(column < HALO, near_piece, plane)
            out_ref[part, first_x + k] = jnp.where(
                column >= HALO + extent_z, far_piece, plane
            )
        return carry

    lax.fori_loop(0, 5 * count_z, unpack_z, 0)
    for copy in moves + x_copies + y_copies + z_copies:
        copy.wait_send()


def gathered(moved, slots, index, kind):
    extent_x, extent_y, extent_z = kind.shape
    planes = extent_x + 2 * HALO
    peers = lax.axis_size("gy")
    blocks = index.shape[0]
    layers = HALO * moved.shape[2] // extent_x
    vmem = pl.BlockSpec(memory_space=pltpu.VMEM)
    smem = pl.BlockSpec(memory_space=pltpu.SMEM)
    tile = (SUBLANES, LANES)
    real = jnp.float32
    return pl.pallas_call(
        gather_kernel,
        out_shape=jax.ShapeDtypeStruct((5, planes) + tile, real),
        in_specs=[vmem, smem, smem, vmem],
        out_specs=vmem,
        scratch_shapes=[
            pltpu.VMEM((peers,) + moved.shape[1:], real),
            pltpu.VMEM((peers,) + moved.shape[1:], real),
            pltpu.VMEM((blocks,) + moved.shape[1:], real),
            pltpu.VMEM((2, blocks, 4, layers), real),
            pltpu.VMEM((extent_x, 2) + tile, real),
            pltpu.VMEM((2, HALO) + tile, real),
            pltpu.VMEM((2, 5 * planes // 6) + tile, real),
            pltpu.VMEM((2, 5 * planes // 6) + tile, real),
            pltpu.VMEM((2, 5 * planes // 8) + tile, real),
            pltpu.VMEM((2, 5 * planes // 8) + tile, real),
            pltpu.SemaphoreType.DMA((peers,)),
            pltpu.SemaphoreType.DMA((peers,)),
            pltpu.SemaphoreType.DMA((8,)),
            pltpu.SemaphoreType.DMA((8,)),
        ],
        compiler_params=pltpu.CompilerParams(
            collective_id=0, has_side_effects=True, vmem_limit_bytes=24 * 1024 * 1024
        ),
        name="gather",
    )(moved, slots, index, kind)


def on_device(moved_fields, send_slot, recv_index, site_kind):
    fields = gathered(
        moved_fields[0, 0, 0],
        send_slot[0, 0, 0].reshape(-1),
        recv_index[0, 0, 0],
        site_kind,
    )
    return lattice(fields, site_kind.shape)


def solution(mesh):
    return jax.shard_map(
        on_device,
        mesh=mesh,
        in_specs=(
            P("gx", "gy", "ba", None, None, None),
            P("gx", "gy", "ba", None, None),
            P("gx", "gy", "ba", None),
            P("gx", "gy", "ba"),
        ),
        out_specs=P(None, "gx", "gy", "ba"),
        check_vma=False,
    )
```

```python
import functools

import jax
import jax.numpy as jnp
from jax import lax
from jax.experimental import pallas as pl
from jax.experimental.pallas import tpu as pltpu
from jax.sharding import PartitionSpec as P

STEPS = 4
HALO = STEPS
PAIRS = (
    (1, 0, 0),
    (0, 1, 0),
    (0, 0, 1),
    (1, 1, 0),
    (1, -1, 0),
    (1, 0, 1),
    (1, 0, -1),
    (0, 1, 1),
    (0, 1, -1),
)
VELOCITIES = ((0, 0, 0),) + tuple(
    tuple(sign * part for part in vector) for vector in PAIRS for sign in (1, -1)
)
WEIGHTS = (1.0 / 3.0,) + (1.0 / 18.0,) * 6 + (1.0 / 36.0,) * 12
RELAX_RATE = 1.25
INLET_SPEED = 0.05
SUBLANES = 8
LANES = 128


def dotted(vector, speeds):
    running = None
    for sign_value, component in zip(vector, speeds):
        if sign_value > 0:
            running = component if running is None else running + component
        elif sign_value < 0:
            running = -component if running is None else running - component
    return running


def row_ids():
    return lax.broadcasted_iota(jnp.int32, (SUBLANES, LANES), 0)


def shifted(plane, rows, stride, step_y, step_z):
    if step_y:
        rolled = pltpu.roll(plane, step_y % SUBLANES, 0)
        crossed = pltpu.roll(rolled, (step_y * stride) % LANES, 1)
        plane = jnp.where(rows == (0 if step_y > 0 else SUBLANES - 1), crossed, rolled)
    if step_z:
        plane = pltpu.roll(plane, step_z % LANES, 1)
    return plane


def unrolled(count, group, body):
    def step(first, carry):
        stores = [entry for k in range(group) for entry in body(first * group + k)]
        for ref, index, value in stores:
            ref[index] = value
        return carry

    lax.fori_loop(0, count // group, step, 0)


def squared_base(speeds):
    return 1.0 - (1.0 / 6.0) * (
        speeds[0] * speeds[0] + speeds[1] * speeds[1] + speeds[2] * speeds[2]
    )


def start_plane(fields, kind):
    wall, inlet = kind == 1.0, kind == 2.0
    factor = jnp.where(kind <= 1.0, fields[0], 1.0)
    scale = jnp.where(wall, -3.0, jnp.where(inlet, 0.0, 3.0))
    speeds = [scale * fields[axis] for axis in (1, 2, 3)]
    speeds[2] = jnp.where(inlet, 3.0 * INLET_SPEED, speeds[2])
    base = squared_base(speeds)
    result = [WEIGHTS[0] * factor * base]
    weighted = {w: w * factor for w in set(WEIGHTS[1:])}
    for pair_id, vector in enumerate(PAIRS):
        w = weighted[WEIGHTS[1 + 2 * pair_id]]
        projected = dotted(vector, speeds)
        even = w * (base + 0.5 * projected * projected)
        odd = w * projected
        result += [even + odd, even - odd]
    return result


def collide_plane(populations, kind):
    fluid, wall, inlet = kind == 0.0, kind == 1.0, kind == 2.0
    sums = [populations[i] + populations[i + 1] for i in range(1, 19, 2)]
    differences = [populations[i] - populations[i + 1] for i in range(1, 19, 2)]
    density = populations[0]
    for member in sums:
        density = density + member
    triple = 3.0 / density
    speeds = []
    for axis in range(3):
        momentum = dotted([vector[axis] for vector in PAIRS], differences)
        speeds.append(jnp.where(wall | inlet, 0.0, momentum * triple))
    speeds[2] = jnp.where(inlet, 3.0 * INLET_SPEED, speeds[2])
    base = squared_base(speeds)
    factor = jnp.where(fluid, RELAX_RATE * density, jnp.where(wall, 0.0, 1.0))
    keep = jnp.where(fluid, 1.0 - RELAX_RATE, jnp.where(wall, 1.0, 0.0))
    half_even = 0.5 * keep
    half_odd = jnp.where(wall, -0.5, half_even)
    result = [keep * populations[0] + WEIGHTS[0] * factor * base]
    weighted = {w: w * factor for w in set(WEIGHTS[1:])}
    for pair_id, vector in enumerate(PAIRS):
        w = weighted[WEIGHTS[1 + 2 * pair_id]]
        projected = dotted(vector, speeds)
        even = half_even * sums[pair_id] + w * (base + 0.5 * projected * projected)
        odd = half_odd * differences[pair_id] + w * projected
        result += [even + odd, even - odd]
    return result


def lattice_kernel(fields_ref, out_ref, first, second):
    planes = fields_ref.shape[1]
    extent_y, extent_z = out_ref.shape[2:]
    stride = extent_z + 2 * HALO
    rows = row_ids()

    def begin(x):
        fields = [fields_ref[i, x] for i in range(5)]
        return [(first, (i, x), m) for i, m in enumerate(start_plane(fields, fields[4]))]

    unrolled(planes, 2, begin)
    source, target = first, second
    for step in range(1, STEPS):

        def advance(x, source=source, target=target, step=step):
            x = x + step
            pulled = [
                shifted(source[i, x - v[0]], rows, stride, v[1], v[2])
                for i, v in enumerate(VELOCITIES)
            ]
            updated = collide_plane(pulled, fields_ref[4, x])
            return [(target, (i, x), member) for i, member in enumerate(updated)]

        unrolled(planes - 2 * step, 2, advance)
        source, target = target, source

    def finish(x):
        stores = []
        for i, v in enumerate(VELOCITIES):
            plane = source[i, x + HALO - v[0]]
            offset = HALO - v[1]
            plane = pltpu.roll(plane, SUBLANES - offset, 0)
            crossed = pltpu.roll(plane, LANES - stride, 1)
            plane = jnp.where(rows < SUBLANES - offset, plane, crossed)
            for group in range(extent_y // SUBLANES):
                part = pltpu.roll(plane, LANES - (group * stride + HALO - v[2]), 1)
                cut = (i, x, pl.ds(group * SUBLANES, SUBLANES), slice(None))
                stores.append((out_ref, cut, part[:, :extent_z]))
        return stores

    unrolled(out_ref.shape[1], 2, finish)


def lattice(fields, extents):
    planes = fields.shape[1]
    return pl.pallas_call(
        lattice_kernel,
        out_shape=jax.ShapeDtypeStruct((19,) + tuple(extents), jnp.float32),
        in_specs=[pl.BlockSpec(memory_space=pltpu.VMEM)],
        out_specs=pl.BlockSpec(memory_space=pltpu.VMEM),
        scratch_shapes=[pltpu.VMEM((19, planes, SUBLANES, LANES), jnp.float32)] * 2,
        compiler_params=pltpu.CompilerParams(vmem_limit_bytes=24 * 1024 * 1024),
        name="lattice",
    )(fields)


def mesh_device(**moved):
    return tuple(moved.get(axis, lax.axis_index(axis)) for axis in ("gx", "gy", "ba"))


def remote(source, target, send_sem, recv_sem, device):
    return pltpu.make_async_remote_copy(
        src_ref=source,
        dst_ref=target,
        send_sem=send_sem,
        recv_sem=recv_sem,
        device_id=device,
        device_id_type=pl.DeviceIdType.MESH,
    )


def grouped(low, high, rows, lanes, stride):
    middle = pltpu.roll(jnp.where(rows < HALO, low, high), stride, 1)
    last = pltpu.roll(high, 2 * stride, 1)
    return jnp.where(lanes < stride, low, jnp.where(lanes < 2 * stride, middle, last))


def gather_kernel(
    moved_in,
    slot_in,
    index_in,
    kind_in,
    out_ref,
    moved_ref,
    slot_ref,
    index_ref,
    kind_ref,
    input_sem,
    staged,
    arrived,
    chosen,
    side_x,
    kind_wide,
    kind_x,
    send_y,
    side_y,
    send_z,
    side_z,
    sent_sem,
    arrived_sem,
    halo_sent,
    halo_arrived,
):
    inputs = [
        pltpu.make_async_copy(source, target, input_sem.at[i])
        for i, (source, target) in enumerate(
            (
                (slot_in, slot_ref),
                (index_in, index_ref),
                (moved_in, moved_ref),
                (kind_in, kind_ref),
            )
        )
    ]
    for copy in inputs:
        copy.start()
    extent_x, extent_y, extent_z = kind_ref.shape
    blocks = chosen.shape[0]
    edge = extent_z // blocks
    stride = extent_z + 2 * HALO
    planes = extent_x + 2 * HALO
    rows = row_ids()
    lanes = lax.broadcasted_iota(jnp.int32, (SUBLANES, LANES), 1)
    me = {axis: lax.axis_index(axis) for axis in ("gx", "gy", "ba")}
    size = {axis: lax.axis_size(axis) for axis in ("gx", "gy", "ba")}
    up = {a: mesh_device(**{a: lax.rem(me[a] + 1, size[a])}) for a in me}
    down = {a: mesh_device(**{a: lax.rem(me[a] + size[a] - 1, size[a])}) for a in me}
    peers = [lax.rem(me["gy"] + offset, size["gy"]) for offset in range(size["gy"])]

    barrier = pltpu.get_barrier_semaphore()
    greeted = [mesh_device(gy=peer) for peer in peers[1:]]
    greeted += [up["gx"], down["gx"], up["ba"], down["ba"]]
    for device in greeted:
        pl.semaphore_signal(
            barrier, inc=1, device_id=device, device_id_type=pl.DeviceIdType.MESH
        )
    for copy in inputs[:3]:
        copy.wait()
    for offset in range(1, size["gy"]):
        staged[offset] = moved_ref[jnp.maximum(slot_ref[peers[offset]], 0)]
    pl.semaphore_wait(barrier, len(greeted))

    moves = []
    for offset in range(1, size["gy"]):
        moves.append(
            remote(
                staged.at[offset],
                arrived.at[me["gy"]],
                sent_sem.at[offset],
                arrived_sem.at[offset],
                mesh_device(gy=peers[offset]),
            )
        )
        moves[-1].start()
    arrived[me["gy"]] = moved_ref[jnp.maximum(slot_ref[me["gy"]], 0)]

    def halo(axis, number, low_source, high_source, target):
        pair = [
            remote(
                high_source,
                target.at[0],
                halo_sent.at[2 * number],
                halo_arrived.at[2 * number],
                up[axis],
            ),
            remote(
                low_source,
                target.at[1],
                halo_sent.at[2 * number + 1],
                halo_arrived.at[2 * number + 1],
                down[axis],
            ),
        ]
        for copy in pair:
            copy.start()
        return pair

    inputs[3].wait()

    def lay_kind(x):
        parts = []
        for half in range(2):
            kind_wide[x, half, :, pl.ds(0, extent_z)] = kind_ref[
                x, pl.ds(half * SUBLANES, SUBLANES), :
            ].astype(jnp.float32)
            wide = pltpu.roll(kind_wide[x, half], HALO, 0)
            parts.append(pltpu.roll(wide, HALO, 1))
        plane = grouped(parts[0], parts[1], rows, lanes, stride)
        return [(out_ref, (4, x + HALO), plane)]

    unrolled(extent_x, 4, lay_kind)
    kind_copies = halo(
        "gx",
        0,
        out_ref.at[4, pl.ds(HALO, HALO)],
        out_ref.at[4, pl.ds(extent_x, HALO)],
        kind_x,
    )

    for move in moves:
        move.wait_recv()
    for block in range(blocks):
        chosen[block] = arrived[index_ref[block]]

    plane_size = edge * edge
    layers = HALO * plane_size
    x_copies = halo(
        "gx",
        1,
        chosen.at[:, :, pl.ds(0, layers)],
        chosen.at[:, :, pl.ds(extent_x * plane_size - layers, layers)],
        side_x,
    )

    def lay_fields(read, x, target_x):
        tiles = []
        for block in range(2):
            for half in range(2):
                start = pl.multiple_of(x * plane_size + half * LANES, LANES)
                tiles.append(read(block, pl.ds(start, LANES)))
        quarter, half_lanes, whole = LANES // 4, LANES // 2, LANES
        stores = []
        for part in range(4):
            picked = []
            for source, tile in enumerate(tiles):
                row = jnp.broadcast_to(tile[part : part + 1], (SUBLANES, LANES))
                turned = pltpu.roll(row, half_lanes, 1)
                low_first = (rows >= HALO) == (source % 2 == 0)
                picked.append(jnp.where(low_first, row, turned))
            pairs = []
            for block in range(2):
                pair = jnp.where(lanes < half_lanes, picked[2 * block], picked[2 * block + 1])
                shift = quarter if block else whole - quarter
                turned = pltpu.roll(pair, shift, 1)
                stays = ((rows & 2) == 0) == (block == 0)
                pairs.append(jnp.where(stays, pair, turned))
            joined = jnp.where((lanes & quarter) == 0, pairs[0], pairs[1])
            joined = jnp.where((rows & 1) == 0, joined, pltpu.roll(joined, whole - edge, 1))
            near = pltpu.roll(joined, HALO, 1)
            far = pltpu.roll(joined, (HALO + edge - quarter) % whole, 1)
            low = jnp.where((lanes & (half_lanes - 1)) < HALO + edge, near, far)
            high = pltpu.roll(low, half_lanes, 1)
            plane = grouped(low, high, rows, lanes, stride)
            stores.append((out_ref, (part, target_x), plane))
        return stores

    def lay_own(x):
        return lay_fields(lambda block, cut: chosen[block, :, cut], x, x + HALO)

    unrolled(extent_x, 4, lay_own)
    for copy in kind_copies:
        copy.wait()
    for copy in x_copies:
        copy.wait_recv()

    for side in range(2):
        first_x = side * (extent_x + HALO)

        def lay_side(x, side=side, first_x=first_x):
            stores = lay_fields(
                lambda block, cut: side_x[side, block, :, cut], x, first_x + x
            )
            return stores + [(out_ref, (4, first_x + x), kind_x[side, x])]

        unrolled(HALO, 4, lay_side)

    per_y = 6
    count_y = planes // per_y

    def pack_y(index):
        stores = []
        part, first_x = index // count_y, (index % count_y) * per_y
        own = [out_ref[part, first_x + k] for k in range(per_y)]
        for side in range(2):
            merged = []
            for half in range(2):
                total = None
                for group in range(3):
                    shift = (group * stride - (0 if side == 0 else 2 * stride)) % LANES
                    piece = own[half * 3 + group]
                    piece = pltpu.roll(piece, shift, 1) if shift else piece
                    total = piece if group == 0 else jnp.where(lanes < group * stride, total, piece)
                merged.append(total)
            other = pltpu.roll(merged[1], HALO, 0)
            keep = rows >= HALO if side == 0 else rows < HALO
            stores.append((send_y, (side, index), jnp.where(keep, merged[0], other)))
        return stores

    unrolled(5 * count_y, 4, pack_y)
    y_copies = halo("gy", 2, send_y.at[0], send_y.at[1], side_y)
    for copy in y_copies:
        copy.wait_recv()

    def unpack_y(index):
        stores = []
        part, first_x = index // count_y, (index % count_y) * per_y
        near = [side_y[0, index], pltpu.roll(side_y[0, index], HALO, 0)]
        far = [side_y[1, index], pltpu.roll(side_y[1, index], HALO, 0)]
        for half in range(2):
            for group in range(3):
                x = first_x + half * 3 + group
                back = (-group * stride) % LANES
                ahead = ((2 - group) * stride) % LANES
                near_piece = pltpu.roll(near[half], back, 1) if back else near[half]
                far_piece = pltpu.roll(far[half], ahead, 1) if ahead else far[half]
                plane = out_ref[part, x]
                plane = jnp.where((rows < HALO) & (lanes < stride), near_piece, plane)
                plane = jnp.where((rows >= HALO) & (lanes >= 2 * stride), far_piece, plane)
                stores.append((out_ref, (part, x), plane))
        return stores

    unrolled(5 * count_y, 4, unpack_y)

    per_z = 8
    count_z = planes // per_z
    column = lax.rem(lanes, stride)

    def pack_z(index):
        stores = []
        part, first_x = index // count_z, (index % count_z) * per_z
        own = [out_ref[part, first_x + k] for k in range(per_z)]
        for side in range(2):
            begin = HALO if side == 0 else extent_z
            total = None
            for k in range(per_z):
                shift = (k * HALO - begin) % LANES
                piece = pltpu.roll(own[k], shift, 1) if shift else own[k]
                total = piece if k == 0 else jnp.where(column < k * HALO, total, piece)
            stores.append((send_z, (side, index), total))
        return stores

    unrolled(5 * count_z, 3, pack_z)
    z_copies = halo("ba", 3, send_z.at[0], send_z.at[1], side_z)
    for copy in z_copies:
        copy.wait_recv()

    def unpack_z(index):
        stores = []
        part, first_x = index // count_z, (index % count_z) * per_z
        near, far = side_z[0, index], side_z[1, index]
        for k in range(per_z):
            back = (-k * HALO) % LANES
            ahead = (HALO + extent_z - k * HALO) % LANES
            near_piece = pltpu.roll(near, back, 1) if back else near
            far_piece = pltpu.roll(far, ahead, 1) if ahead else far
            plane = out_ref[part, first_x + k]
            plane = jnp.where(column < HALO, near_piece, plane)
            plane = jnp.where(column >= HALO + extent_z, far_piece, plane)
            stores.append((out_ref, (part, first_x + k), plane))
        return stores

    unrolled(5 * count_z, 3, unpack_z)
    for copy in moves + x_copies + y_copies + z_copies:
        copy.wait_send()


def gathered(moved, slots, index, kind):
    extent_x, extent_y, extent_z = kind.shape
    planes = extent_x + 2 * HALO
    peers = lax.axis_size("gy")
    blocks = index.shape[0]
    layers = HALO * moved.shape[2] // extent_x
    vmem = pl.BlockSpec(memory_space=pltpu.VMEM)
    anywhere = pl.BlockSpec(memory_space=pltpu.HBM)
    tile = (SUBLANES, LANES)
    real = jnp.float32
    return pl.pallas_call(
        gather_kernel,
        out_shape=jax.ShapeDtypeStruct((5, planes) + tile, real),
        in_specs=[anywhere] * 4,
        out_specs=vmem,
        scratch_shapes=[
            pltpu.VMEM(moved.shape, real),
            pltpu.SMEM(slots.shape, jnp.int32),
            pltpu.SMEM(index.shape, jnp.int32),
            pltpu.VMEM(kind.shape, jnp.int32),
            pltpu.SemaphoreType.DMA((4,)),
            pltpu.VMEM((peers,) + moved.shape[1:], real),
            pltpu.VMEM((peers,) + moved.shape[1:], real),
            pltpu.VMEM((blocks,) + moved.shape[1:], real),
            pltpu.VMEM((2, blocks, 4, layers), real),
            pltpu.VMEM((extent_x, 2) + tile, real),
            pltpu.VMEM((2, HALO) + tile, real),
            pltpu.VMEM((2, 5 * planes // 6) + tile, real),
            pltpu.VMEM((2, 5 * planes // 6) + tile, real),
            pltpu.VMEM((2, 5 * planes // 8) + tile, real),
            pltpu.VMEM((2, 5 * planes // 8) + tile, real),
            pltpu.SemaphoreType.DMA((peers,)),
            pltpu.SemaphoreType.DMA((peers,)),
            pltpu.SemaphoreType.DMA((8,)),
            pltpu.SemaphoreType.DMA((8,)),
        ],
        compiler_params=pltpu.CompilerParams(
            collective_id=0, has_side_effects=True, vmem_limit_bytes=60 * 1024 * 1024
        ),
        name="gather",
    )(moved, slots, index, kind)


def on_device(moved_fields, send_slot, recv_index, site_kind):
    fields = gathered(
        moved_fields[0, 0, 0],
        send_slot[0, 0, 0].reshape(-1),
        recv_index[0, 0, 0],
        site_kind,
    )
    return lattice(fields, site_kind.shape)


def solution(mesh):
    return jax.shard_map(
        on_device,
        mesh=mesh,
        in_specs=(
            P("gx", "gy", "ba", None, None, None),
            P("gx", "gy", "ba", None, None),
            P("gx", "gy", "ba", None),
            P("gx", "gy", "ba"),
        ),
        out_specs=P(None, "gx", "gy", "ba"),
        check_vma=False,
    )
```

```python
import functools

import jax
import jax.numpy as jnp
from jax import lax
from jax.experimental import pallas as pl
from jax.experimental.pallas import tpu as pltpu
from jax.sharding import PartitionSpec as P

STEPS = 4
HALO = STEPS
PAIRS = (
    (1, 0, 0),
    (0, 1, 0),
    (0, 0, 1),
    (1, 1, 0),
    (1, -1, 0),
    (1, 0, 1),
    (1, 0, -1),
    (0, 1, 1),
    (0, 1, -1),
)
VELOCITIES = ((0, 0, 0),) + tuple(
    tuple(sign * part for part in vector) for vector in PAIRS for sign in (1, -1)
)
WEIGHTS = (1.0 / 3.0,) + (1.0 / 18.0,) * 6 + (1.0 / 36.0,) * 12
RELAX_RATE = 1.25
INLET_SPEED = 0.05
SUBLANES = 8
LANES = 128


def dotted(vector, speeds):
    running = None
    for sign_value, component in zip(vector, speeds):
        if sign_value > 0:
            running = component if running is None else running + component
        elif sign_value < 0:
            running = -component if running is None else running - component
    return running


def row_ids():
    return lax.broadcasted_iota(jnp.int32, (SUBLANES, LANES), 0)


def shifted(plane, rows, stride, step_y, step_z):
    if step_y:
        rolled = pltpu.roll(plane, step_y % SUBLANES, 0)
        crossed = pltpu.roll(rolled, (step_y * stride) % LANES, 1)
        plane = jnp.where(rows == (0 if step_y > 0 else SUBLANES - 1), crossed, rolled)
    if step_z:
        plane = pltpu.roll(plane, step_z % LANES, 1)
    return plane


def unrolled(count, group, body):
    def step(first, carry):
        stores = [entry for k in range(group) for entry in body(first * group + k)]
        for ref, index, value in stores:
            ref[index] = value
        return carry

    lax.fori_loop(0, count // group, step, 0)


def squared_base(speeds):
    return 1.0 - (1.0 / 6.0) * (
        speeds[0] * speeds[0] + speeds[1] * speeds[1] + speeds[2] * speeds[2]
    )


def start_plane(fields, kind):
    wall, inlet = kind == 1.0, kind == 2.0
    factor = jnp.where(kind <= 1.0, fields[0], 1.0)
    scale = jnp.where(wall, -3.0, jnp.where(inlet, 0.0, 3.0))
    speeds = [scale * fields[axis] for axis in (1, 2, 3)]
    speeds[2] = jnp.where(inlet, 3.0 * INLET_SPEED, speeds[2])
    base = squared_base(speeds)
    result = [WEIGHTS[0] * factor * base]
    weighted = {w: w * factor for w in set(WEIGHTS[1:])}
    for pair_id, vector in enumerate(PAIRS):
        w = weighted[WEIGHTS[1 + 2 * pair_id]]
        projected = dotted(vector, speeds)
        even = w * (base + 0.5 * projected * projected)
        odd = w * projected
        result += [even + odd, even - odd]
    return result


def collide_plane(populations, kind):
    fluid, wall, inlet = kind == 0.0, kind == 1.0, kind == 2.0
    sums = [populations[i] + populations[i + 1] for i in range(1, 19, 2)]
    differences = [populations[i] - populations[i + 1] for i in range(1, 19, 2)]
    density = populations[0]
    for member in sums:
        density = density + member
    triple = 3.0 / density
    speeds = []
    for axis in range(3):
        momentum = dotted([vector[axis] for vector in PAIRS], differences)
        speeds.append(jnp.where(wall | inlet, 0.0, momentum * triple))
    speeds[2] = jnp.where(inlet, 3.0 * INLET_SPEED, speeds[2])
    base = squared_base(speeds)
    factor = jnp.where(fluid, RELAX_RATE * density, jnp.where(wall, 0.0, 1.0))
    keep = jnp.where(fluid, 1.0 - RELAX_RATE, jnp.where(wall, 1.0, 0.0))
    half_even = 0.5 * keep
    half_odd = jnp.where(wall, -0.5, half_even)
    result = [keep * populations[0] + WEIGHTS[0] * factor * base]
    weighted = {w: w * factor for w in set(WEIGHTS[1:])}
    for pair_id, vector in enumerate(PAIRS):
        w = weighted[WEIGHTS[1 + 2 * pair_id]]
        projected = dotted(vector, speeds)
        even = half_even * sums[pair_id] + w * (base + 0.5 * projected * projected)
        odd = half_odd * differences[pair_id] + w * projected
        result += [even + odd, even - odd]
    return result


def lattice_kernel(fields_in, out, fields_ref, result, first, second, in_sem, out_sem):
    planes = fields_ref.shape[1]
    extent_x, extent_y, extent_z = out.shape[1:]
    count = in_sem.shape[0]
    cuts = [pl.ds(i * (planes // count), planes // count) for i in range(count)]
    loads = [
        pltpu.make_async_copy(fields_in.at[:, cut], fields_ref.at[:, cut], in_sem.at[i])
        for i, cut in enumerate(cuts)
    ]
    for load in loads:
        load.start()
    stride = extent_z + 2 * HALO
    rows = row_ids()

    def begin(x, offset):
        x = x + offset
        fields = [fields_ref[i, x] for i in range(5)]
        return [(first, (i, x), m) for i, m in enumerate(start_plane(fields, fields[4]))]

    for i, load in enumerate(loads):
        load.wait()
        unrolled(
            planes // count, 2, functools.partial(begin, offset=i * (planes // count))
        )
    source, target = first, second
    for step in range(1, STEPS):

        def advance(x, source=source, target=target, step=step):
            x = x + step
            pulled = [
                shifted(source[i, x - v[0]], rows, stride, v[1], v[2])
                for i, v in enumerate(VELOCITIES)
            ]
            updated = collide_plane(pulled, fields_ref[4, x])
            return [(target, (i, x), member) for i, member in enumerate(updated)]

        unrolled(planes - 2 * step, 2, advance)
        source, target = target, source

    def finish(x, offset):
        x = x + offset
        stores = []
        for i, v in enumerate(VELOCITIES):
            plane = source[i, x + HALO - v[0]]
            offset = HALO - v[1]
            plane = pltpu.roll(plane, SUBLANES - offset, 0)
            crossed = pltpu.roll(plane, LANES - stride, 1)
            plane = jnp.where(rows < SUBLANES - offset, plane, crossed)
            for group in range(extent_y // SUBLANES):
                part = pltpu.roll(plane, LANES - (group * stride + HALO - v[2]), 1)
                cut = (i, x, pl.ds(group * SUBLANES, SUBLANES), slice(None))
                stores.append((result, cut, part[:, :extent_z]))
        return stores

    count = out_sem.shape[0]
    saves = []
    for i in range(count):
        length = extent_x // count
        unrolled(length, 2, functools.partial(finish, offset=i * length))
        cut = pl.ds(i * length, length)
        saves.append(
            pltpu.make_async_copy(result.at[:, cut], out.at[:, cut], out_sem.at[i])
        )
        saves[-1].start()
    for save in saves:
        save.wait()


def lattice(fields, extents):
    planes = fields.shape[1]
    return pl.pallas_call(
        lattice_kernel,
        out_shape=jax.ShapeDtypeStruct((19,) + tuple(extents), jnp.float32),
        in_specs=[pl.BlockSpec(memory_space=pltpu.HBM)],
        out_specs=pl.BlockSpec(memory_space=pltpu.HBM),
        scratch_shapes=[
            pltpu.VMEM(fields.shape, jnp.float32),
            pltpu.VMEM((19,) + tuple(extents), jnp.float32),
            pltpu.VMEM((19, planes, SUBLANES, LANES), jnp.float32),
            pltpu.VMEM((19, planes, SUBLANES, LANES), jnp.float32),
            pltpu.SemaphoreType.DMA((4,)),
            pltpu.SemaphoreType.DMA((4,)),
        ],
        compiler_params=pltpu.CompilerParams(vmem_limit_bytes=60 * 1024 * 1024),
        name="lattice",
    )(fields)


def mesh_device(**moved):
    return tuple(moved.get(axis, lax.axis_index(axis)) for axis in ("gx", "gy", "ba"))


def remote(source, target, send_sem, recv_sem, device):
    return pltpu.make_async_remote_copy(
        src_ref=source,
        dst_ref=target,
        send_sem=send_sem,
        recv_sem=recv_sem,
        device_id=device,
        device_id_type=pl.DeviceIdType.MESH,
    )


def grouped(low, high, rows, lanes, stride):
    middle = pltpu.roll(jnp.where(rows < HALO, low, high), stride, 1)
    last = pltpu.roll(high, 2 * stride, 1)
    return jnp.where(lanes < stride, low, jnp.where(lanes < 2 * stride, middle, last))


def gather_kernel(
    moved_in,
    slot_in,
    index_in,
    kind_in,
    out_ref,
    moved_ref,
    slot_ref,
    index_ref,
    kind_ref,
    input_sem,
    staged,
    arrived,
    chosen,
    side_x,
    kind_wide,
    kind_x,
    send_y,
    recv_y,
    send_z,
    side_z,
    sent_sem,
    arrived_sem,
    halo_sent,
    halo_arrived,
):
    inputs = [
        pltpu.make_async_copy(source, target, input_sem.at[i])
        for i, (source, target) in enumerate(
            (
                (slot_in, slot_ref),
                (index_in, index_ref),
                (moved_in, moved_ref),
                (kind_in, kind_ref),
            )
        )
    ]
    for copy in inputs:
        copy.start()
    extent_x, extent_y, extent_z = kind_ref.shape
    blocks = chosen.shape[0]
    edge = extent_z // blocks
    stride = extent_z + 2 * HALO
    planes = extent_x + 2 * HALO
    rows = row_ids()
    lanes = lax.broadcasted_iota(jnp.int32, (SUBLANES, LANES), 1)
    me = {axis: lax.axis_index(axis) for axis in ("gx", "gy", "ba")}
    size = {axis: lax.axis_size(axis) for axis in ("gx", "gy", "ba")}
    up = {a: mesh_device(**{a: lax.rem(me[a] + 1, size[a])}) for a in me}
    down = {a: mesh_device(**{a: lax.rem(me[a] + size[a] - 1, size[a])}) for a in me}
    peers = [lax.rem(me["gy"] + offset, size["gy"]) for offset in range(size["gy"])]

    barrier = pltpu.get_barrier_semaphore()
    greeted = [mesh_device(gy=peer) for peer in peers[1:]]
    greeted += [up["gx"], down["gx"], up["ba"], down["ba"]]
    ahead_x, ahead_y = (lax.rem(me[a] + 1, size[a]) for a in ("gx", "gy"))
    behind_x, behind_y = (lax.rem(me[a] + size[a] - 1, size[a]) for a in ("gx", "gy"))
    corners = [
        [mesh_device(gx=x, gy=y) for x in (behind_x, ahead_x)] for y in (behind_y, ahead_y)
    ]
    greeted += corners[0] + corners[1]
    for device in greeted:
        pl.semaphore_signal(
            barrier, inc=1, device_id=device, device_id_type=pl.DeviceIdType.MESH
        )
    for copy in inputs[:3]:
        copy.wait()
    for offset in range(1, size["gy"]):
        staged[offset] = moved_ref[jnp.maximum(slot_ref[peers[offset]], 0)]
    pl.semaphore_wait(barrier, len(greeted))

    moves = []
    for offset in range(1, size["gy"]):
        moves.append(
            remote(
                staged.at[offset],
                arrived.at[me["gy"]],
                sent_sem.at[offset],
                arrived_sem.at[offset],
                mesh_device(gy=peers[offset]),
            )
        )
        moves[-1].start()
    arrived[me["gy"]] = moved_ref[jnp.maximum(slot_ref[me["gy"]], 0)]

    def halo(axis, number, low_source, high_source, target):
        pair = [
            remote(
                high_source,
                target.at[0],
                halo_sent.at[2 * number],
                halo_arrived.at[2 * number],
                up[axis],
            ),
            remote(
                low_source,
                target.at[1],
                halo_sent.at[2 * number + 1],
                halo_arrived.at[2 * number + 1],
                down[axis],
            ),
        ]
        for copy in pair:
            copy.start()
        return pair

    quad_lanes = LANES // HALO
    quads = extent_x // HALO

    def pack_y(pair, quad):
        stores = []
        for side in range(2):
            merged = []
            for half in range(2):
                part = min(2 * pair + half, 4)
                total = None
                for k in range(HALO):
                    begin = HALO + (0 if side == 0 else 2 * stride)
                    piece = out_ref[part, quad * HALO + HALO + k]
                    piece = pltpu.roll(piece, (k * quad_lanes - begin) % LANES, 1)
                    total = piece if k == 0 else jnp.where(lanes < k * quad_lanes, total, piece)
                merged.append(total)
            other = pltpu.roll(merged[1], HALO, 0)
            keep = rows >= HALO if side == 0 else rows < HALO
            stores.append((send_y, (side, quad, pair), jnp.where(keep, merged[0], other)))
        return stores

    def unpack_y(pair, quad):
        stores = []
        near, far = recv_y[0, quad, pair], recv_y[1, quad, pair]
        for half in range(1 if pair == 2 else 2):
            part = 2 * pair + half
            if half:
                near, far = pltpu.roll(near, HALO, 0), pltpu.roll(far, HALO, 0)
            for k in range(HALO):
                x = quad * HALO + k
                near_piece = pltpu.roll(near, (HALO - k * quad_lanes) % LANES, 1)
                far_piece = pltpu.roll(
                    far, (HALO + 2 * stride - k * quad_lanes) % LANES, 1
                )
                plane = out_ref[part, x]
                plane = jnp.where((rows < HALO) & (lanes < stride), near_piece, plane)
                plane = jnp.where((rows >= HALO) & (lanes >= 2 * stride), far_piece, plane)
                stores.append((out_ref, (part, x), plane))
        return stores

    def halo_y(first, pairs):
        copies = []
        for toward in range(2):
            send, land = toward, 1 - toward
            routes = (
                ((up if toward else down)["gy"], pl.ds(0, quads), pl.ds(1, quads)),
                (corners[toward][1], pl.ds(quads - 1, 1), pl.ds(0, 1)),
                (corners[toward][0], pl.ds(0, 1), pl.ds(quads + 1, 1)),
            )
            for number, (device, source, target) in enumerate(routes):
                sem = first + toward * 3 + number
                copies.append(
                    remote(
                        send_y.at[send, source, pairs],
                        recv_y.at[land, target, pairs],
                        halo_sent.at[sem],
                        halo_arrived.at[sem],
                        device,
                    )
                )
                copies[-1].start()
        return copies

    inputs[3].wait()

    def lay_kind(x):
        parts = []
        for half in range(2):
            kind_wide[x, half, :, pl.ds(0, extent_z)] = kind_ref[
                x, pl.ds(half * SUBLANES, SUBLANES), :
            ].astype(jnp.float32)
            wide = pltpu.roll(kind_wide[x, half], HALO, 0)
            parts.append(pltpu.roll(wide, HALO, 1))
        plane = grouped(parts[0], parts[1], rows, lanes, stride)
        return [(out_ref, (4, x + HALO), plane)]

    unrolled(extent_x, 4, lay_kind)
    kind_copies = halo(
        "gx",
        0,
        out_ref.at[4, pl.ds(HALO, HALO)],
        out_ref.at[4, pl.ds(extent_x, HALO)],
        kind_x,
    )
    unrolled(quads, 4, lambda quad: pack_y(2, quad))
    kind_y = halo_y(12, pl.ds(2, 1))

    for move in moves:
        move.wait_recv()
    for block in range(blocks):
        chosen[block] = arrived[index_ref[block]]

    plane_size = edge * edge
    layers = HALO * plane_size
    x_copies = halo(
        "gx",
        1,
        chosen.at[:, :, pl.ds(0, layers)],
        chosen.at[:, :, pl.ds(extent_x * plane_size - layers, layers)],
        side_x,
    )

    def lay_fields(read, x, target_x):
        tiles = []
        for block in range(2):
            for half in range(2):
                start = pl.multiple_of(x * plane_size + half * LANES, LANES)
                tiles.append(read(block, pl.ds(start, LANES)))
        quarter, half_lanes, whole = LANES // 4, LANES // 2, LANES
        stores = []
        for part in range(4):
            picked = []
            for source, tile in enumerate(tiles):
                row = jnp.broadcast_to(tile[part : part + 1], (SUBLANES, LANES))
                turned = pltpu.roll(row, half_lanes, 1)
                low_first = (rows >= HALO) == (source % 2 == 0)
                picked.append(jnp.where(low_first, row, turned))
            pairs = []
            for block in range(2):
                pair = jnp.where(lanes < half_lanes, picked[2 * block], picked[2 * block + 1])
                shift = quarter if block else whole - quarter
                turned = pltpu.roll(pair, shift, 1)
                stays = ((rows & 2) == 0) == (block == 0)
                pairs.append(jnp.where(stays, pair, turned))
            joined = jnp.where((lanes & quarter) == 0, pairs[0], pairs[1])
            joined = jnp.where((rows & 1) == 0, joined, pltpu.roll(joined, whole - edge, 1))
            near = pltpu.roll(joined, HALO, 1)
            far = pltpu.roll(joined, (HALO + edge - quarter) % whole, 1)
            low = jnp.where((lanes & (half_lanes - 1)) < HALO + edge, near, far)
            high = pltpu.roll(low, half_lanes, 1)
            plane = grouped(low, high, rows, lanes, stride)
            stores.append((out_ref, (part, target_x), plane))
        return stores

    def lay_own(x):
        return lay_fields(lambda block, cut: chosen[block, :, cut], x, x + HALO)

    unrolled(extent_x, 4, lay_own)
    for pair in range(2):
        unrolled(quads, 4, lambda quad, pair=pair: pack_y(pair, quad))
    y_copies = halo_y(6, pl.ds(0, 2))
    for copy in kind_copies:
        copy.wait()
    for copy in x_copies:
        copy.wait_recv()

    for side in range(2):
        first_x = side * (extent_x + HALO)

        def lay_side(x, side=side, first_x=first_x):
            stores = lay_fields(
                lambda block, cut: side_x[side, block, :, cut], x, first_x + x
            )
            return stores + [(out_ref, (4, first_x + x), kind_x[side, x])]

        unrolled(HALO, 4, lay_side)

    for copy in y_copies + kind_y:
        copy.wait_recv()
    for pair in range(3):
        unrolled(quads + 2, 3, lambda quad, pair=pair: unpack_y(pair, quad))

    per_z = 8
    count_z = planes // per_z
    column = lax.rem(lanes, stride)

    def pack_z(index):
        stores = []
        part, first_x = index // count_z, (index % count_z) * per_z
        own = [out_ref[part, first_x + k] for k in range(per_z)]
        for side in range(2):
            begin = HALO if side == 0 else extent_z
            total = None
            for k in range(per_z):
                shift = (k * HALO - begin) % LANES
                piece = pltpu.roll(own[k], shift, 1) if shift else own[k]
                total = piece if k == 0 else jnp.where(column < k * HALO, total, piece)
            stores.append((send_z, (side, index), total))
        return stores

    unrolled(5 * count_z, 3, pack_z)
    z_copies = halo("ba", 2, send_z.at[0], send_z.at[1], side_z)
    for copy in z_copies:
        copy.wait_recv()

    def unpack_z(index):
        stores = []
        part, first_x = index // count_z, (index % count_z) * per_z
        near, far = side_z[0, index], side_z[1, index]
        for k in range(per_z):
            back = (-k * HALO) % LANES
            ahead = (HALO + extent_z - k * HALO) % LANES
            near_piece = pltpu.roll(near, back, 1) if back else near
            far_piece = pltpu.roll(far, ahead, 1) if ahead else far
            plane = out_ref[part, first_x + k]
            plane = jnp.where(column < HALO, near_piece, plane)
            plane = jnp.where(column >= HALO + extent_z, far_piece, plane)
            stores.append((out_ref, (part, first_x + k), plane))
        return stores

    unrolled(5 * count_z, 3, unpack_z)
    for copy in moves + x_copies + y_copies + kind_y + z_copies:
        copy.wait_send()


def gathered(moved, slots, index, kind):
    extent_x, extent_y, extent_z = kind.shape
    planes = extent_x + 2 * HALO
    peers = lax.axis_size("gy")
    blocks = index.shape[0]
    layers = HALO * moved.shape[2] // extent_x
    vmem = pl.BlockSpec(memory_space=pltpu.VMEM)
    anywhere = pl.BlockSpec(memory_space=pltpu.HBM)
    tile = (SUBLANES, LANES)
    real = jnp.float32
    return pl.pallas_call(
        gather_kernel,
        out_shape=jax.ShapeDtypeStruct((5, planes) + tile, real),
        in_specs=[anywhere] * 4,
        out_specs=vmem,
        scratch_shapes=[
            pltpu.VMEM(moved.shape, real),
            pltpu.SMEM(slots.shape, jnp.int32),
            pltpu.SMEM(index.shape, jnp.int32),
            pltpu.VMEM(kind.shape, jnp.int32),
            pltpu.SemaphoreType.DMA((4,)),
            pltpu.VMEM((peers,) + moved.shape[1:], real),
            pltpu.VMEM((peers,) + moved.shape[1:], real),
            pltpu.VMEM((blocks,) + moved.shape[1:], real),
            pltpu.VMEM((2, blocks, 4, layers), real),
            pltpu.VMEM((extent_x, 2) + tile, real),
            pltpu.VMEM((2, HALO) + tile, real),
            pltpu.VMEM((2, extent_x // HALO, 3) + tile, real),
            pltpu.VMEM((2, extent_x // HALO + 2, 3) + tile, real),
            pltpu.VMEM((2, 5 * planes // 8) + tile, real),
            pltpu.VMEM((2, 5 * planes // 8) + tile, real),
            pltpu.SemaphoreType.DMA((peers,)),
            pltpu.SemaphoreType.DMA((peers,)),
            pltpu.SemaphoreType.DMA((18,)),
            pltpu.SemaphoreType.DMA((18,)),
        ],
        compiler_params=pltpu.CompilerParams(
            collective_id=0, has_side_effects=True, vmem_limit_bytes=60 * 1024 * 1024
        ),
        name="gather",
    )(moved, slots, index, kind)


def on_device(moved_fields, send_slot, recv_index, site_kind):
    fields = gathered(
        moved_fields[0, 0, 0],
        send_slot[0, 0, 0].reshape(-1),
        recv_index[0, 0, 0],
        site_kind,
    )
    return lattice(fields, site_kind.shape)


def solution(mesh):
    return jax.shard_map(
        on_device,
        mesh=mesh,
        in_specs=(
            P("gx", "gy", "ba", None, None, None),
            P("gx", "gy", "ba", None, None),
            P("gx", "gy", "ba", None),
            P("gx", "gy", "ba"),
        ),
        out_specs=P(None, "gx", "gy", "ba"),
        check_vma=False,
    )
```

```python
import functools

import jax
import jax.numpy as jnp
from jax import lax
from jax.experimental import pallas as pl
from jax.experimental.pallas import tpu as pltpu
from jax.sharding import PartitionSpec as P

STEPS = 4
HALO = STEPS
PAIRS = (
    (1, 0, 0),
    (0, 1, 0),
    (0, 0, 1),
    (1, 1, 0),
    (1, -1, 0),
    (1, 0, 1),
    (1, 0, -1),
    (0, 1, 1),
    (0, 1, -1),
)
VELOCITIES = ((0, 0, 0),) + tuple(
    tuple(sign * part for part in vector) for vector in PAIRS for sign in (1, -1)
)
WEIGHTS = (1.0 / 3.0,) + (1.0 / 18.0,) * 6 + (1.0 / 36.0,) * 12
RELAX_RATE = 1.25
INLET_SPEED = 0.05
SUBLANES = 8
LANES = 128


def dotted(vector, speeds):
    running = None
    for sign_value, component in zip(vector, speeds):
        if sign_value > 0:
            running = component if running is None else running + component
        elif sign_value < 0:
            running = -component if running is None else running - component
    return running


def row_ids():
    return lax.broadcasted_iota(jnp.int32, (SUBLANES, LANES), 0)


def shifted(plane, rows, stride, step_y, step_z):
    if step_y:
        rolled = pltpu.roll(plane, step_y % SUBLANES, 0)
        crossed = pltpu.roll(rolled, (step_y * stride) % LANES, 1)
        plane = jnp.where(rows == (0 if step_y > 0 else SUBLANES - 1), crossed, rolled)
    if step_z:
        plane = pltpu.roll(plane, step_z % LANES, 1)
    return plane


def unrolled(count, group, body):
    def several(sites):
        stores = [entry for site in sites for entry in body(site)]
        for ref, index, value in stores:
            ref[index] = value

    def step(first, carry):
        several([first * group + k for k in range(group)])
        return carry

    whole = count // group
    if whole > 1:
        lax.fori_loop(0, whole, step, 0)
    elif whole:
        several(range(group))
    if count % group:
        several(range(whole * group, count))


def squared_base(speeds):
    return 1.0 - (1.0 / 6.0) * (
        speeds[0] * speeds[0] + speeds[1] * speeds[1] + speeds[2] * speeds[2]
    )


def start_plane(fields, kind):
    wall, inlet = kind == 1.0, kind == 2.0
    factor = jnp.where(kind <= 1.0, fields[0], 1.0)
    scale = jnp.where(wall, -3.0, jnp.where(inlet, 0.0, 3.0))
    speeds = [scale * fields[axis] for axis in (1, 2, 3)]
    speeds[2] = jnp.where(inlet, 3.0 * INLET_SPEED, speeds[2])
    base = squared_base(speeds)
    result = [WEIGHTS[0] * factor * base]
    weighted = {w: w * factor for w in set(WEIGHTS[1:])}
    for pair_id, vector in enumerate(PAIRS):
        w = weighted[WEIGHTS[1 + 2 * pair_id]]
        projected = dotted(vector, speeds)
        even = w * (base + 0.5 * projected * projected)
        odd = w * projected
        result += [even + odd, even - odd]
    return result


def collide_plane(populations, kind):
    fluid, wall, inlet = kind == 0.0, kind == 1.0, kind == 2.0
    sums = [populations[i] + populations[i + 1] for i in range(1, 19, 2)]
    differences = [populations[i] - populations[i + 1] for i in range(1, 19, 2)]
    density = populations[0]
    for member in sums:
        density = density + member
    triple = 3.0 / density
    speeds = []
    for axis in range(3):
        momentum = dotted([vector[axis] for vector in PAIRS], differences)
        speeds.append(jnp.where(wall | inlet, 0.0, momentum * triple))
    speeds[2] = jnp.where(inlet, 3.0 * INLET_SPEED, speeds[2])
    base = squared_base(speeds)
    factor = jnp.where(fluid, RELAX_RATE * density, jnp.where(wall, 0.0, 1.0))
    keep = jnp.where(fluid, 1.0 - RELAX_RATE, jnp.where(wall, 1.0, 0.0))
    half_even = 0.5 * keep
    half_odd = jnp.where(wall, -0.5, half_even)
    result = [keep * populations[0] + WEIGHTS[0] * factor * base]
    weighted = {w: w * factor for w in set(WEIGHTS[1:])}
    for pair_id, vector in enumerate(PAIRS):
        w = weighted[WEIGHTS[1 + 2 * pair_id]]
        projected = dotted(vector, speeds)
        even = half_even * sums[pair_id] + w * (base + 0.5 * projected * projected)
        odd = half_odd * differences[pair_id] + w * projected
        result += [even + odd, even - odd]
    return result


def lattice_kernel(fields_in, out, fields_ref, result, first, second, in_sem, out_sem):
    planes = fields_ref.shape[1]
    extent_x, extent_y, extent_z = out.shape[1:]
    count = in_sem.shape[0]
    cuts = [pl.ds(i * (planes // count), planes // count) for i in range(count)]
    loads = [
        pltpu.make_async_copy(fields_in.at[:, cut], fields_ref.at[:, cut], in_sem.at[i])
        for i, cut in enumerate(cuts)
    ]
    for load in loads:
        load.start()
    stride = extent_z + 2 * HALO
    rows = row_ids()

    def begin(x, offset):
        x = x + offset
        fields = [fields_ref[i, x] for i in range(5)]
        return [(first, (i, x), m) for i, m in enumerate(start_plane(fields, fields[4]))]

    for i, load in enumerate(loads):
        load.wait()
        unrolled(
            planes // count, 3, functools.partial(begin, offset=i * (planes // count))
        )
    source, target = first, second
    for step in range(1, STEPS):

        def advance(x, source=source, target=target, step=step):
            x = x + step
            pulled = [
                shifted(source[i, x - v[0]], rows, stride, v[1], v[2])
                for i, v in enumerate(VELOCITIES)
            ]
            updated = collide_plane(pulled, fields_ref[4, x])
            return [(target, (i, x), member) for i, member in enumerate(updated)]

        unrolled(planes - 2 * step, 4, advance)
        source, target = target, source

    def finish(x, offset):
        x = x + offset
        stores = []
        for i, v in enumerate(VELOCITIES):
            plane = source[i, x + HALO - v[0]]
            offset = HALO - v[1]
            plane = pltpu.roll(plane, SUBLANES - offset, 0)
            crossed = pltpu.roll(plane, LANES - stride, 1)
            plane = jnp.where(rows < SUBLANES - offset, plane, crossed)
            for group in range(extent_y // SUBLANES):
                part = pltpu.roll(plane, LANES - (group * stride + HALO - v[2]), 1)
                cut = (i, x, pl.ds(group * SUBLANES, SUBLANES), slice(None))
                stores.append((result, cut, part[:, :extent_z]))
        return stores

    count = out_sem.shape[0]
    saves = []
    for i in range(count):
        length = extent_x // count
        unrolled(length, 4, functools.partial(finish, offset=i * length))
        cut = pl.ds(i * length, length)
        saves.append(
            pltpu.make_async_copy(result.at[:, cut], out.at[:, cut], out_sem.at[i])
        )
        saves[-1].start()
    for save in saves:
        save.wait()


def lattice(fields, extents):
    planes = fields.shape[1]
    return pl.pallas_call(
        lattice_kernel,
        out_shape=jax.ShapeDtypeStruct((19,) + tuple(extents), jnp.float32),
        in_specs=[pl.BlockSpec(memory_space=pltpu.HBM)],
        out_specs=pl.BlockSpec(memory_space=pltpu.HBM),
        scratch_shapes=[
            pltpu.VMEM(fields.shape, jnp.float32),
            pltpu.VMEM((19,) + tuple(extents), jnp.float32),
            pltpu.VMEM((19, planes, SUBLANES, LANES), jnp.float32),
            pltpu.VMEM((19, planes, SUBLANES, LANES), jnp.float32),
            pltpu.SemaphoreType.DMA((4,)),
            pltpu.SemaphoreType.DMA((4,)),
        ],
        compiler_params=pltpu.CompilerParams(vmem_limit_bytes=60 * 1024 * 1024),
        name="lattice",
    )(fields)


def mesh_device(**moved):
    return tuple(moved.get(axis, lax.axis_index(axis)) for axis in ("gx", "gy", "ba"))


def remote(source, target, send_sem, recv_sem, device):
    return pltpu.make_async_remote_copy(
        src_ref=source,
        dst_ref=target,
        send_sem=send_sem,
        recv_sem=recv_sem,
        device_id=device,
        device_id_type=pl.DeviceIdType.MESH,
    )


def grouped(low, high, rows, lanes, stride):
    middle = pltpu.roll(jnp.where(rows < HALO, low, high), stride, 1)
    last = pltpu.roll(high, 2 * stride, 1)
    return jnp.where(lanes < stride, low, jnp.where(lanes < 2 * stride, middle, last))


def gather_kernel(
    moved_in,
    slot_in,
    index_in,
    kind_in,
    out_ref,
    moved_ref,
    slot_ref,
    index_ref,
    kind_ref,
    input_sem,
    staged,
    arrived_low,
    arrived_high,
    arrived_mid,
    chosen_low,
    chosen_high,
    chosen_mid,
    side_x,
    kind_wide,
    kind_x,
    send_y,
    recv_y,
    send_z,
    side_z,
    sent_sem,
    arrived_sem,
    halo_sent,
    halo_arrived,
):
    inputs = [
        pltpu.make_async_copy(source, target, input_sem.at[i])
        for i, (source, target) in enumerate(
            (
                (slot_in, slot_ref),
                (index_in, index_ref),
                (moved_in, moved_ref),
                (kind_in, kind_ref),
            )
        )
    ]
    for copy in inputs:
        copy.start()
    extent_x, extent_y, extent_z = kind_ref.shape
    blocks = chosen_low.shape[0]
    edge = extent_z // blocks
    stride = extent_z + 2 * HALO
    planes = extent_x + 2 * HALO
    rows = row_ids()
    lanes = lax.broadcasted_iota(jnp.int32, (SUBLANES, LANES), 1)
    me = {axis: lax.axis_index(axis) for axis in ("gx", "gy", "ba")}
    size = {axis: lax.axis_size(axis) for axis in ("gx", "gy", "ba")}
    up = {a: mesh_device(**{a: lax.rem(me[a] + 1, size[a])}) for a in me}
    down = {a: mesh_device(**{a: lax.rem(me[a] + size[a] - 1, size[a])}) for a in me}
    peers = [lax.rem(me["gy"] + offset, size["gy"]) for offset in range(size["gy"])]

    barrier = pltpu.get_barrier_semaphore()
    greeted = [mesh_device(gy=peer) for peer in peers[1:]]
    greeted += [up["gx"], down["gx"], up["ba"], down["ba"]]
    ahead_x, ahead_y = (lax.rem(me[a] + 1, size[a]) for a in ("gx", "gy"))
    behind_x, behind_y = (lax.rem(me[a] + size[a] - 1, size[a]) for a in ("gx", "gy"))
    corners = [
        [mesh_device(gx=x, gy=y) for x in (behind_x, ahead_x)] for y in (behind_y, ahead_y)
    ]
    greeted += corners[0] + corners[1]
    for device in greeted:
        pl.semaphore_signal(
            barrier, inc=1, device_id=device, device_id_type=pl.DeviceIdType.MESH
        )
    for copy in inputs[:3]:
        copy.wait()
    for offset in range(1, size["gy"]):
        staged[offset] = moved_ref[jnp.maximum(slot_ref[peers[offset]], 0)]
    pl.semaphore_wait(barrier, len(greeted))

    plane_size = moved_ref.shape[2] // extent_x
    layers = HALO * plane_size
    pieces = (
        (arrived_low, 0, layers),
        (arrived_high, extent_x * plane_size - layers, layers),
        (arrived_mid, layers, extent_x * plane_size - 2 * layers),
    )
    moves = []
    for number, (target, begin, length) in enumerate(pieces):
        moves.append([])
        for offset in range(1, size["gy"]):
            copy = remote(
                staged.at[offset, :, pl.ds(begin, length)],
                target.at[me["gy"]],
                sent_sem.at[number, offset],
                arrived_sem.at[number, offset],
                mesh_device(gy=peers[offset]),
            )
            copy.start()
            moves[-1].append(copy)
    own_slot = jnp.maximum(slot_ref[me["gy"]], 0)
    for target, begin, length in pieces:
        target[me["gy"]] = moved_ref[own_slot, :, pl.ds(begin, length)]

    def halo(axis, number, low_source, high_source, target):
        pair = [
            remote(
                high_source,
                target.at[0],
                halo_sent.at[2 * number],
                halo_arrived.at[2 * number],
                up[axis],
            ),
            remote(
                low_source,
                target.at[1],
                halo_sent.at[2 * number + 1],
                halo_arrived.at[2 * number + 1],
                down[axis],
            ),
        ]
        for copy in pair:
            copy.start()
        return pair

    quad_lanes = LANES // HALO
    quads = extent_x // HALO

    def pack_y(pair, quad):
        stores = []
        for side in range(2):
            merged = []
            for half in range(2):
                part = min(2 * pair + half, 4)
                total = None
                for k in range(HALO):
                    begin = HALO + (0 if side == 0 else 2 * stride)
                    piece = out_ref[part, quad * HALO + HALO + k]
                    piece = pltpu.roll(piece, (k * quad_lanes - begin) % LANES, 1)
                    total = piece if k == 0 else jnp.where(lanes < k * quad_lanes, total, piece)
                merged.append(total)
            other = pltpu.roll(merged[1], HALO, 0)
            keep = rows >= HALO if side == 0 else rows < HALO
            stores.append((send_y, (side, quad, pair), jnp.where(keep, merged[0], other)))
        return stores

    def unpack_y(pair, quad):
        stores = []
        near, far = recv_y[0, quad, pair], recv_y[1, quad, pair]
        for half in range(1 if pair == 2 else 2):
            part = 2 * pair + half
            if half:
                near, far = pltpu.roll(near, HALO, 0), pltpu.roll(far, HALO, 0)
            for k in range(HALO):
                x = quad * HALO + k
                near_piece = pltpu.roll(near, (HALO - k * quad_lanes) % LANES, 1)
                far_piece = pltpu.roll(
                    far, (HALO + 2 * stride - k * quad_lanes) % LANES, 1
                )
                plane = out_ref[part, x]
                plane = jnp.where((rows < HALO) & (lanes < stride), near_piece, plane)
                plane = jnp.where((rows >= HALO) & (lanes >= 2 * stride), far_piece, plane)
                stores.append((out_ref, (part, x), plane))
        return stores

    last = quads - 1
    outer_y = (
        ("straight", 0, 1, 1),
        ("straight", last, 1, last + 1),
        ("ahead", last, 1, 0),
        ("behind", 0, 1, quads + 1),
    )
    inner_y = (("straight", 1, quads - 2, 2),)
    whole_y = (("straight", 0, quads, 1),) + outer_y[2:]

    def halo_y(first, pairs, routes):
        copies = []
        for toward in range(2):
            devices = {
                "straight": (up if toward else down)["gy"],
                "behind": corners[toward][0],
                "ahead": corners[toward][1],
            }
            for route, source, length, target in routes:
                sem = first + len(copies)
                copies.append(
                    remote(
                        send_y.at[toward, pl.ds(source, length), pairs],
                        recv_y.at[1 - toward, pl.ds(target, length), pairs],
                        halo_sent.at[sem],
                        halo_arrived.at[sem],
                        devices[route],
                    )
                )
                copies[-1].start()
        return copies

    inputs[3].wait()

    def lay_kind(x):
        parts = []
        for half in range(2):
            kind_wide[x, half, :, pl.ds(0, extent_z)] = kind_ref[
                x, pl.ds(half * SUBLANES, SUBLANES), :
            ].astype(jnp.float32)
            wide = pltpu.roll(kind_wide[x, half], HALO, 0)
            parts.append(pltpu.roll(wide, HALO, 1))
        plane = grouped(parts[0], parts[1], rows, lanes, stride)
        return [(out_ref, (4, x + HALO), plane)]

    unrolled(extent_x, 4, lay_kind)
    kind_copies = halo(
        "gx",
        0,
        out_ref.at[4, pl.ds(HALO, HALO)],
        out_ref.at[4, pl.ds(extent_x, HALO)],
        kind_x,
    )
    unrolled(quads, 4, lambda quad: pack_y(2, quad))
    kind_y = halo_y(18, pl.ds(2, 1), whole_y)

    def choose(number, target):
        for copy in moves[number]:
            copy.wait_recv()
        for block in range(blocks):
            target[block] = pieces[number][0][index_ref[block]]

    def lay_fields(read, x, target_x):
        tiles = []
        for block in range(2):
            for half in range(2):
                start = pl.multiple_of(x * plane_size + half * LANES, LANES)
                tiles.append(read(block, pl.ds(start, LANES)))
        quarter, half_lanes, whole = LANES // 4, LANES // 2, LANES
        stores = []
        for part in range(4):
            picked = []
            for source, tile in enumerate(tiles):
                row = jnp.broadcast_to(tile[part : part + 1], (SUBLANES, LANES))
                turned = pltpu.roll(row, half_lanes, 1)
                low_first = (rows >= HALO) == (source % 2 == 0)
                picked.append(jnp.where(low_first, row, turned))
            pairs = []
            for block in range(2):
                pair = jnp.where(lanes < half_lanes, picked[2 * block], picked[2 * block + 1])
                shift = quarter if block else whole - quarter
                turned = pltpu.roll(pair, shift, 1)
                stays = ((rows & 2) == 0) == (block == 0)
                pairs.append(jnp.where(stays, pair, turned))
            joined = jnp.where((lanes & quarter) == 0, pairs[0], pairs[1])
            joined = jnp.where((rows & 1) == 0, joined, pltpu.roll(joined, whole - edge, 1))
            near = pltpu.roll(joined, HALO, 1)
            far = pltpu.roll(joined, (HALO + edge - quarter) % whole, 1)
            low = jnp.where((lanes & (half_lanes - 1)) < HALO + edge, near, far)
            high = pltpu.roll(low, half_lanes, 1)
            plane = grouped(low, high, rows, lanes, stride)
            stores.append((out_ref, (part, target_x), plane))
        return stores

    def lay_own(source, count, first_x):
        def lay(x):
            return lay_fields(lambda block, cut: source[block, :, cut], x, first_x + x)

        unrolled(count, 4, lay)

    choose(0, chosen_low)
    choose(1, chosen_high)
    x_copies = halo("gx", 1, chosen_low, chosen_high, side_x)
    lay_own(chosen_low, HALO, HALO)
    lay_own(chosen_high, HALO, extent_x)
    for pair in range(2):
        unrolled(2, 2, lambda k, pair=pair: pack_y(pair, k * last))
    outer_copies = halo_y(8, pl.ds(0, 2), outer_y)
    for copy in kind_copies:
        copy.wait()
    for copy in x_copies:
        copy.wait_recv()

    for side in range(2):
        first_x = side * (extent_x + HALO)

        def lay_side(x, side=side, first_x=first_x):
            stores = lay_fields(
                lambda block, cut: side_x[side, block, :, cut], x, first_x + x
            )
            return stores + [(out_ref, (4, first_x + x), kind_x[side, x])]

        unrolled(HALO, 4, lay_side)

    choose(2, chosen_mid)
    lay_own(chosen_mid, extent_x - 2 * HALO, 2 * HALO)
    for pair in range(2):
        unrolled(quads - 2, 2, lambda k, pair=pair: pack_y(pair, 1 + k))
    inner_copies = halo_y(16, pl.ds(0, 2), inner_y)

    per_z = 8
    count_z = planes // per_z
    column = lax.rem(lanes, stride)

    def pack_z(part, slot):
        stores = []
        first_x = group_z[slot] * per_z
        own = [out_ref[part, first_x + k] for k in range(per_z)]
        for side in range(2):
            begin = HALO if side == 0 else extent_z
            total = None
            for k in range(per_z):
                shift = (k * HALO - begin) % LANES
                piece = pltpu.roll(own[k], shift, 1) if shift else own[k]
                total = piece if k == 0 else jnp.where(column < k * HALO, total, piece)
            stores.append((send_z, (side, slot, part), total))
        return stores

    def unpack_z(part, slot):
        stores = []
        first_x = group_z[slot] * per_z
        near, far = side_z[0, slot, part], side_z[1, slot, part]
        for k in range(per_z):
            back = (-k * HALO) % LANES
            ahead = (HALO + extent_z - k * HALO) % LANES
            near_piece = pltpu.roll(near, back, 1) if back else near
            far_piece = pltpu.roll(far, ahead, 1) if ahead else far
            plane = out_ref[part, first_x + k]
            plane = jnp.where(column < HALO, near_piece, plane)
            plane = jnp.where(column >= HALO + extent_z, far_piece, plane)
            stores.append((out_ref, (part, first_x + k), plane))
        return stores

    def exchange_z(number, slots):
        for slot in slots:
            unrolled(5, 5, lambda part, slot=slot: pack_z(part, slot))
        cut = pl.ds(slots[0], len(slots))
        return halo("ba", number, send_z.at[0, cut], send_z.at[1, cut], side_z.at[:, cut])

    group_z = [0] + [count_z - 1] + list(range(1, count_z - 1))
    for copy in outer_copies + kind_y:
        copy.wait_recv()
    for pair in range(3):
        unrolled(2, 2, lambda k, pair=pair: unpack_y(pair, k))
        unrolled(2, 2, lambda k, pair=pair: unpack_y(pair, quads + k))
    outer_z = exchange_z(2, [0, 1])
    for copy in inner_copies:
        copy.wait_recv()
    for pair in range(3):
        unrolled(2, 2, lambda k, pair=pair: unpack_y(pair, 2 + k))
    inner_z = exchange_z(3, list(range(2, count_z)))
    for copies, slots in ((outer_z, [0, 1]), (inner_z, list(range(2, count_z)))):
        for copy in copies:
            copy.wait_recv()
        for slot in slots:
            unrolled(5, 5, lambda part, slot=slot: unpack_z(part, slot))
    sent = moves[0] + moves[1] + moves[2] + x_copies + kind_y
    for copy in sent + outer_copies + inner_copies + outer_z + inner_z:
        copy.wait_send()


def gathered(moved, slots, index, kind):
    extent_x, extent_y, extent_z = kind.shape
    planes = extent_x + 2 * HALO
    peers = lax.axis_size("gy")
    blocks = index.shape[0]
    layers = HALO * moved.shape[2] // extent_x
    vmem = pl.BlockSpec(memory_space=pltpu.VMEM)
    anywhere = pl.BlockSpec(memory_space=pltpu.HBM)
    tile = (SUBLANES, LANES)
    real = jnp.float32
    return pl.pallas_call(
        gather_kernel,
        out_shape=jax.ShapeDtypeStruct((5, planes) + tile, real),
        in_specs=[anywhere] * 4,
        out_specs=vmem,
        scratch_shapes=[
            pltpu.VMEM(moved.shape, real),
            pltpu.SMEM(slots.shape, jnp.int32),
            pltpu.SMEM(index.shape, jnp.int32),
            pltpu.VMEM(kind.shape, jnp.int32),
            pltpu.SemaphoreType.DMA((4,)),
            pltpu.VMEM((peers,) + moved.shape[1:], real),
            pltpu.VMEM((peers, 4, layers), real),
            pltpu.VMEM((peers, 4, layers), real),
            pltpu.VMEM((peers, 4, moved.shape[2] - 2 * layers), real),
            pltpu.VMEM((blocks, 4, layers), real),
            pltpu.VMEM((blocks, 4, layers), real),
            pltpu.VMEM((blocks, 4, moved.shape[2] - 2 * layers), real),
            pltpu.VMEM((2, blocks, 4, layers), real),
            pltpu.VMEM((extent_x, 2) + tile, real),
            pltpu.VMEM((2, HALO) + tile, real),
            pltpu.VMEM((2, extent_x // HALO, 3) + tile, real),
            pltpu.VMEM((2, extent_x // HALO + 2, 3) + tile, real),
            pltpu.VMEM((2, planes // 8, 5) + tile, real),
            pltpu.VMEM((2, planes // 8, 5) + tile, real),
            pltpu.SemaphoreType.DMA((3, peers)),
            pltpu.SemaphoreType.DMA((3, peers)),
            pltpu.SemaphoreType.DMA((24,)),
            pltpu.SemaphoreType.DMA((24,)),
        ],
        compiler_params=pltpu.CompilerParams(
            collective_id=0, has_side_effects=True, vmem_limit_bytes=60 * 1024 * 1024
        ),
        name="gather",
    )(moved, slots, index, kind)


def on_device(moved_fields, send_slot, recv_index, site_kind):
    fields = gathered(
        moved_fields[0, 0, 0],
        send_slot[0, 0, 0].reshape(-1),
        recv_index[0, 0, 0],
        site_kind,
    )
    return lattice(fields, site_kind.shape)


def solution(mesh):
    return jax.shard_map(
        on_device,
        mesh=mesh,
        in_specs=(
            P("gx", "gy", "ba", None, None, None),
            P("gx", "gy", "ba", None, None),
            P("gx", "gy", "ba", None),
            P("gx", "gy", "ba"),
        ),
        out_specs=P(None, "gx", "gy", "ba"),
        check_vma=False,
    )
```

```python
import functools

import jax
import jax.numpy as jnp
from jax import lax
from jax.experimental import pallas as pl
from jax.experimental.pallas import tpu as pltpu
from jax.sharding import PartitionSpec as P

STEPS = 4
HALO = STEPS
PAIRS = (
    (1, 0, 0),
    (0, 1, 0),
    (0, 0, 1),
    (1, 1, 0),
    (1, -1, 0),
    (1, 0, 1),
    (1, 0, -1),
    (0, 1, 1),
    (0, 1, -1),
)
VELOCITIES = ((0, 0, 0),) + tuple(
    tuple(sign * part for part in vector) for vector in PAIRS for sign in (1, -1)
)
WEIGHTS = (1.0 / 3.0,) + (1.0 / 18.0,) * 6 + (1.0 / 36.0,) * 12
RELAX_RATE = 1.25
INLET_SPEED = 0.05
SUBLANES = 8
LANES = 128


def dotted(vector, speeds):
    running = None
    for sign_value, component in zip(vector, speeds):
        if sign_value > 0:
            running = component if running is None else running + component
        elif sign_value < 0:
            running = -component if running is None else running - component
    return running


def row_ids():
    return lax.broadcasted_iota(jnp.int32, (SUBLANES, LANES), 0)


def shifted(plane, rows, stride, step_y, step_z):
    if step_y:
        rolled = pltpu.roll(plane, step_y % SUBLANES, 0)
        crossed = pltpu.roll(rolled, (step_y * stride) % LANES, 1)
        plane = jnp.where(rows == (0 if step_y > 0 else SUBLANES - 1), crossed, rolled)
    if step_z:
        plane = pltpu.roll(plane, step_z % LANES, 1)
    return plane


def unrolled(count, group, body, before=None, after=None):
    def several(sites):
        stores = [entry for site in sites for entry in body(site)]
        for ref, index, value in stores:
            ref[index] = value

    def step(first, carry):
        if before is not None:
            before(first)
        several([first * group + k for k in range(group)])
        if after is not None:
            after(first)
        return carry

    whole = count // group
    if whole > 1:
        lax.fori_loop(0, whole, step, 0)
    elif whole:
        several(range(group))
    if count % group:
        several(range(whole * group, count))


def squared_base(speeds):
    return 1.0 - (1.0 / 6.0) * (
        speeds[0] * speeds[0] + speeds[1] * speeds[1] + speeds[2] * speeds[2]
    )


def start_plane(fields, kind):
    wall, inlet = kind == 1.0, kind == 2.0
    factor = jnp.where(kind <= 1.0, fields[0], 1.0)
    scale = jnp.where(wall, -3.0, jnp.where(inlet, 0.0, 3.0))
    speeds = [scale * fields[axis] for axis in (1, 2, 3)]
    speeds[2] = jnp.where(inlet, 3.0 * INLET_SPEED, speeds[2])
    base = squared_base(speeds)
    result = [WEIGHTS[0] * factor * base]
    weighted = {w: w * factor for w in set(WEIGHTS[1:])}
    for pair_id, vector in enumerate(PAIRS):
        w = weighted[WEIGHTS[1 + 2 * pair_id]]
        projected = dotted(vector, speeds)
        even = w * (base + 0.5 * projected * projected)
        odd = w * projected
        result += [even + odd, even - odd]
    return result


def collide_plane(populations, kind):
    fluid, wall, inlet = kind == 0.0, kind == 1.0, kind == 2.0
    sums = [populations[i] + populations[i + 1] for i in range(1, 19, 2)]
    differences = [populations[i] - populations[i + 1] for i in range(1, 19, 2)]
    density = populations[0]
    for member in sums:
        density = density + member
    triple = 3.0 / density
    speeds = []
    for axis in range(3):
        momentum = dotted([vector[axis] for vector in PAIRS], differences)
        speeds.append(jnp.where(wall | inlet, 0.0, momentum * triple))
    speeds[2] = jnp.where(inlet, 3.0 * INLET_SPEED, speeds[2])
    base = squared_base(speeds)
    factor = jnp.where(fluid, RELAX_RATE * density, jnp.where(wall, 0.0, 1.0))
    keep = jnp.where(fluid, 1.0 - RELAX_RATE, jnp.where(wall, 1.0, 0.0))
    half_even = 0.5 * keep
    half_odd = jnp.where(wall, -0.5, half_even)
    result = [keep * populations[0] + WEIGHTS[0] * factor * base]
    weighted = {w: w * factor for w in set(WEIGHTS[1:])}
    for pair_id, vector in enumerate(PAIRS):
        w = weighted[WEIGHTS[1 + 2 * pair_id]]
        projected = dotted(vector, speeds)
        even = half_even * sums[pair_id] + w * (base + 0.5 * projected * projected)
        odd = half_odd * differences[pair_id] + w * projected
        result += [even + odd, even - odd]
    return result


def lattice_kernel(fields_in, out, fields_ref, result, first, second, in_sem, out_sem):
    planes = fields_ref.shape[1]
    extent_x, extent_y, extent_z = out.shape[1:]

    def load(i):
        cut = pl.ds(2 * i, 2)
        return pltpu.make_async_copy(fields_in.at[:, cut], fields_ref.at[:, cut], in_sem.at[i])

    def save(i):
        cut = pl.ds(2 * i, 2)
        return pltpu.make_async_copy(result.at[:, cut], out.at[:, cut], out_sem.at[i])

    for i in range(planes // 2):
        load(i).start()
    stride = extent_z + 2 * HALO
    rows = row_ids()

    def begin(x):
        fields = [fields_ref[i, x] for i in range(5)]
        return [(first, (i, x), m) for i, m in enumerate(start_plane(fields, fields[4]))]

    unrolled(planes, 2, begin, before=lambda i: load(i).wait())
    source, target = first, second
    for step in range(1, STEPS):

        def advance(x, source=source, target=target, step=step):
            x = x + step
            pulled = [
                shifted(source[i, x - v[0]], rows, stride, v[1], v[2])
                for i, v in enumerate(VELOCITIES)
            ]
            updated = collide_plane(pulled, fields_ref[4, x])
            return [(target, (i, x), member) for i, member in enumerate(updated)]

        unrolled(planes - 2 * step, 2, advance)
        source, target = target, source

    def finish(x):
        stores = []
        for i, v in enumerate(VELOCITIES):
            plane = source[i, x + HALO - v[0]]
            offset = HALO - v[1]
            plane = pltpu.roll(plane, SUBLANES - offset, 0)
            crossed = pltpu.roll(plane, LANES - stride, 1)
            plane = jnp.where(rows < SUBLANES - offset, plane, crossed)
            for group in range(extent_y // SUBLANES):
                part = pltpu.roll(plane, LANES - (group * stride + HALO - v[2]), 1)
                cut = (i, x, pl.ds(group * SUBLANES, SUBLANES), slice(None))
                stores.append((result, cut, part[:, :extent_z]))
        return stores

    unrolled(extent_x, 2, finish, after=lambda i: save(i).start())
    for i in range(extent_x // 2):
        save(i).wait()


def lattice(fields, extents):
    planes = fields.shape[1]
    return pl.pallas_call(
        lattice_kernel,
        out_shape=jax.ShapeDtypeStruct((19,) + tuple(extents), jnp.float32),
        in_specs=[pl.BlockSpec(memory_space=pltpu.HBM)],
        out_specs=pl.BlockSpec(memory_space=pltpu.HBM),
        scratch_shapes=[
            pltpu.VMEM(fields.shape, jnp.float32),
            pltpu.VMEM((19,) + tuple(extents), jnp.float32),
            pltpu.VMEM((19, planes, SUBLANES, LANES), jnp.float32),
            pltpu.VMEM((19, planes, SUBLANES, LANES), jnp.float32),
            pltpu.SemaphoreType.DMA((planes // 2,)),
            pltpu.SemaphoreType.DMA((extents[0] // 2,)),
        ],
        compiler_params=pltpu.CompilerParams(vmem_limit_bytes=60 * 1024 * 1024),
        name="lattice",
    )(fields)


def mesh_device(**moved):
    return tuple(moved.get(axis, lax.axis_index(axis)) for axis in ("gx", "gy", "ba"))


def remote(source, target, send_sem, recv_sem, device):
    return pltpu.make_async_remote_copy(
        src_ref=source,
        dst_ref=target,
        send_sem=send_sem,
        recv_sem=recv_sem,
        device_id=device,
        device_id_type=pl.DeviceIdType.MESH,
    )


def grouped(low, high, rows, lanes, stride):
    middle = pltpu.roll(jnp.where(rows < HALO, low, high), stride, 1)
    last = pltpu.roll(high, 2 * stride, 1)
    return jnp.where(lanes < stride, low, jnp.where(lanes < 2 * stride, middle, last))


def gather_kernel(
    moved_in,
    slot_in,
    index_in,
    kind_in,
    out_ref,
    moved_ref,
    slot_ref,
    index_ref,
    kind_ref,
    input_sem,
    staged,
    arrived_low,
    arrived_high,
    arrived_mid,
    chosen_low,
    chosen_high,
    chosen_mid,
    side_x,
    kind_wide,
    kind_x,
    send_y,
    recv_y,
    send_z,
    side_z,
    sent_sem,
    arrived_sem,
    halo_sent,
    halo_arrived,
):
    inputs = [
        pltpu.make_async_copy(source, target, input_sem.at[i])
        for i, (source, target) in enumerate(
            (
                (slot_in, slot_ref),
                (index_in, index_ref),
                (moved_in, moved_ref),
                (kind_in, kind_ref),
            )
        )
    ]
    for copy in inputs:
        copy.start()
    extent_x, extent_y, extent_z = kind_ref.shape
    blocks = chosen_low.shape[0]
    edge = extent_z // blocks
    stride = extent_z + 2 * HALO
    planes = extent_x + 2 * HALO
    rows = row_ids()
    lanes = lax.broadcasted_iota(jnp.int32, (SUBLANES, LANES), 1)
    me = {axis: lax.axis_index(axis) for axis in ("gx", "gy", "ba")}
    size = {axis: lax.axis_size(axis) for axis in ("gx", "gy", "ba")}
    up = {a: mesh_device(**{a: lax.rem(me[a] + 1, size[a])}) for a in me}
    down = {a: mesh_device(**{a: lax.rem(me[a] + size[a] - 1, size[a])}) for a in me}
    peers = [lax.rem(me["gy"] + offset, size["gy"]) for offset in range(size["gy"])]

    barrier = pltpu.get_barrier_semaphore()
    greeted = [mesh_device(gy=peer) for peer in peers[1:]]
    greeted += [up["gx"], down["gx"], up["ba"], down["ba"]]
    ahead_x, ahead_y = (lax.rem(me[a] + 1, size[a]) for a in ("gx", "gy"))
    behind_x, behind_y = (lax.rem(me[a] + size[a] - 1, size[a]) for a in ("gx", "gy"))
    corners = [
        [mesh_device(gx=x, gy=y) for x in (behind_x, ahead_x)] for y in (behind_y, ahead_y)
    ]
    greeted += corners[0] + corners[1]
    for device in greeted:
        pl.semaphore_signal(
            barrier, inc=1, device_id=device, device_id_type=pl.DeviceIdType.MESH
        )
    for copy in inputs[:3]:
        copy.wait()
    for offset in range(1, size["gy"]):
        staged[offset] = moved_ref[jnp.maximum(slot_ref[peers[offset]], 0)]
    pl.semaphore_wait(barrier, len(greeted))

    plane_size = moved_ref.shape[2] // extent_x
    layers = HALO * plane_size
    pieces = (
        (arrived_low, 0, layers),
        (arrived_high, extent_x * plane_size - layers, layers),
        (arrived_mid, layers, extent_x * plane_size - 2 * layers),
    )
    moves = []
    for number, (target, begin, length) in enumerate(pieces):
        moves.append([])
        for offset in range(1, size["gy"]):
            copy = remote(
                staged.at[offset, :, pl.ds(begin, length)],
                target.at[me["gy"]],
                sent_sem.at[number, offset],
                arrived_sem.at[number, offset],
                mesh_device(gy=peers[offset]),
            )
            copy.start()
            moves[-1].append(copy)
    own_slot = jnp.maximum(slot_ref[me["gy"]], 0)
    for target, begin, length in pieces:
        target[me["gy"]] = moved_ref[own_slot, :, pl.ds(begin, length)]

    def halo(axis, number, low_source, high_source, target):
        pair = [
            remote(
                high_source,
                target.at[0],
                halo_sent.at[2 * number],
                halo_arrived.at[2 * number],
                up[axis],
            ),
            remote(
                low_source,
                target.at[1],
                halo_sent.at[2 * number + 1],
                halo_arrived.at[2 * number + 1],
                down[axis],
            ),
        ]
        for copy in pair:
            copy.start()
        return pair

    quad_lanes = LANES // HALO
    quads = extent_x // HALO

    def pack_y(pair, quad):
        stores = []
        for side in range(2):
            merged = []
            for half in range(2):
                part = min(2 * pair + half, 4)
                total = None
                for k in range(HALO):
                    begin = HALO + (0 if side == 0 else 2 * stride)
                    piece = out_ref[part, quad * HALO + HALO + k]
                    piece = pltpu.roll(piece, (k * quad_lanes - begin) % LANES, 1)
                    total = piece if k == 0 else jnp.where(lanes < k * quad_lanes, total, piece)
                merged.append(total)
            other = pltpu.roll(merged[1], HALO, 0)
            keep = rows >= HALO if side == 0 else rows < HALO
            stores.append((send_y, (side, quad, pair), jnp.where(keep, merged[0], other)))
        return stores

    def unpack_y(pair, quad):
        stores = []
        near, far = recv_y[0, quad, pair], recv_y[1, quad, pair]
        for half in range(1 if pair == 2 else 2):
            part = 2 * pair + half
            if half:
                near, far = pltpu.roll(near, HALO, 0), pltpu.roll(far, HALO, 0)
            for k in range(HALO):
                x = quad * HALO + k
                near_piece = pltpu.roll(near, (HALO - k * quad_lanes) % LANES, 1)
                far_piece = pltpu.roll(
                    far, (HALO + 2 * stride - k * quad_lanes) % LANES, 1
                )
                plane = out_ref[part, x]
                plane = jnp.where((rows < HALO) & (lanes < stride), near_piece, plane)
                plane = jnp.where((rows >= HALO) & (lanes >= 2 * stride), far_piece, plane)
                stores.append((out_ref, (part, x), plane))
        return stores

    last = quads - 1
    outer_y = (
        ("straight", 0, 1, 1),
        ("straight", last, 1, last + 1),
        ("ahead", last, 1, 0),
        ("behind", 0, 1, quads + 1),
    )
    inner_y = (("straight", 1, quads - 2, 2),)
    whole_y = (("straight", 0, quads, 1),) + outer_y[2:]

    def halo_y(first, pairs, routes):
        copies = []
        for toward in range(2):
            devices = {
                "straight": (up if toward else down)["gy"],
                "behind": corners[toward][0],
                "ahead": corners[toward][1],
            }
            for route, source, length, target in routes:
                sem = first + len(copies)
                copies.append(
                    remote(
                        send_y.at[toward, pl.ds(source, length), pairs],
                        recv_y.at[1 - toward, pl.ds(target, length), pairs],
                        halo_sent.at[sem],
                        halo_arrived.at[sem],
                        devices[route],
                    )
                )
                copies[-1].start()
        return copies

    inputs[3].wait()

    def lay_kind(x):
        parts = []
        for half in range(2):
            kind_wide[x, half, :, pl.ds(0, extent_z)] = kind_ref[
                x, pl.ds(half * SUBLANES, SUBLANES), :
            ].astype(jnp.float32)
            wide = pltpu.roll(kind_wide[x, half], HALO, 0)
            parts.append(pltpu.roll(wide, HALO, 1))
        plane = grouped(parts[0], parts[1], rows, lanes, stride)
        return [(out_ref, (4, x + HALO), plane)]

    unrolled(extent_x, 4, lay_kind)
    kind_copies = halo(
        "gx",
        0,
        out_ref.at[4, pl.ds(HALO, HALO)],
        out_ref.at[4, pl.ds(extent_x, HALO)],
        kind_x,
    )
    unrolled(quads, 4, lambda quad: pack_y(2, quad))
    kind_y = halo_y(18, pl.ds(2, 1), whole_y)

    def choose(number, target):
        for copy in moves[number]:
            copy.wait_recv()
        for block in range(blocks):
            target[block] = pieces[number][0][index_ref[block]]

    def lay_fields(read, x, target_x):
        tiles = []
        for block in range(2):
            for half in range(2):
                start = pl.multiple_of(x * plane_size + half * LANES, LANES)
                tiles.append(read(block, pl.ds(start, LANES)))
        quarter, half_lanes, whole = LANES // 4, LANES // 2, LANES
        stores = []
        for part in range(4):
            picked = []
            for source, tile in enumerate(tiles):
                row = jnp.broadcast_to(tile[part : part + 1], (SUBLANES, LANES))
                turned = pltpu.roll(row, half_lanes, 1)
                low_first = (rows >= HALO) == (source % 2 == 0)
                picked.append(jnp.where(low_first, row, turned))
            pairs = []
            for block in range(2):
                pair = jnp.where(lanes < half_lanes, picked[2 * block], picked[2 * block + 1])
                shift = quarter if block else whole - quarter
                turned = pltpu.roll(pair, shift, 1)
                stays = ((rows & 2) == 0) == (block == 0)
                pairs.append(jnp.where(stays, pair, turned))
            joined = jnp.where((lanes & quarter) == 0, pairs[0], pairs[1])
            joined = jnp.where((rows & 1) == 0, joined, pltpu.roll(joined, whole - edge, 1))
            near = pltpu.roll(joined, HALO, 1)
            far = pltpu.roll(joined, (HALO + edge - quarter) % whole, 1)
            low = jnp.where((lanes & (half_lanes - 1)) < HALO + edge, near, far)
            high = pltpu.roll(low, half_lanes, 1)
            plane = grouped(low, high, rows, lanes, stride)
            stores.append((out_ref, (part, target_x), plane))
        return stores

    def lay_own(source, count, first_x):
        def lay(x):
            return lay_fields(lambda block, cut: source[block, :, cut], x, first_x + x)

        unrolled(count, 4, lay)

    choose(0, chosen_low)
    choose(1, chosen_high)
    x_copies = halo("gx", 1, chosen_low, chosen_high, side_x)
    lay_own(chosen_low, HALO, HALO)
    lay_own(chosen_high, HALO, extent_x)
    for pair in range(2):
        unrolled(2, 2, lambda k, pair=pair: pack_y(pair, k * last))
    outer_copies = halo_y(8, pl.ds(0, 2), outer_y)
    for copy in kind_copies:
        copy.wait()
    for copy in x_copies:
        copy.wait_recv()

    for side in range(2):
        first_x = side * (extent_x + HALO)

        def lay_side(x, side=side, first_x=first_x):
            stores = lay_fields(
                lambda block, cut: side_x[side, block, :, cut], x, first_x + x
            )
            return stores + [(out_ref, (4, first_x + x), kind_x[side, x])]

        unrolled(HALO, 4, lay_side)

    choose(2, chosen_mid)
    lay_own(chosen_mid, extent_x - 2 * HALO, 2 * HALO)
    for pair in range(2):
        unrolled(quads - 2, 2, lambda k, pair=pair: pack_y(pair, 1 + k))
    inner_copies = halo_y(16, pl.ds(0, 2), inner_y)

    per_z = 8
    count_z = planes // per_z
    column = lax.rem(lanes, stride)

    def pack_z(part, slot):
        stores = []
        first_x = group_z[slot] * per_z
        own = [out_ref[part, first_x + k] for k in range(per_z)]
        for side in range(2):
            begin = HALO if side == 0 else extent_z
            total = None
            for k in range(per_z):
                shift = (k * HALO - begin) % LANES
                piece = pltpu.roll(own[k], shift, 1) if shift else own[k]
                total = piece if k == 0 else jnp.where(column < k * HALO, total, piece)
            stores.append((send_z, (side, slot, part), total))
        return stores

    def unpack_z(part, slot):
        stores = []
        first_x = group_z[slot] * per_z
        near, far = side_z[0, slot, part], side_z[1, slot, part]
        for k in range(per_z):
            back = (-k * HALO) % LANES
            ahead = (HALO + extent_z - k * HALO) % LANES
            near_piece = pltpu.roll(near, back, 1) if back else near
            far_piece = pltpu.roll(far, ahead, 1) if ahead else far
            plane = out_ref[part, first_x + k]
            plane = jnp.where(column < HALO, near_piece, plane)
            plane = jnp.where(column >= HALO + extent_z, far_piece, plane)
            stores.append((out_ref, (part, first_x + k), plane))
        return stores

    def exchange_z(number, slots):
        for slot in slots:
            unrolled(5, 5, lambda part, slot=slot: pack_z(part, slot))
        cut = pl.ds(slots[0], len(slots))
        return halo("ba", number, send_z.at[0, cut], send_z.at[1, cut], side_z.at[:, cut])

    group_z = [0] + [count_z - 1] + list(range(1, count_z - 1))
    for copy in outer_copies + kind_y:
        copy.wait_recv()
    for pair in range(3):
        unrolled(2, 2, lambda k, pair=pair: unpack_y(pair, k))
        unrolled(2, 2, lambda k, pair=pair: unpack_y(pair, quads + k))
    outer_z = exchange_z(2, [0, 1])
    for copy in inner_copies:
        copy.wait_recv()
    for pair in range(3):
        unrolled(2, 2, lambda k, pair=pair: unpack_y(pair, 2 + k))
    inner_z = exchange_z(3, list(range(2, count_z)))
    for copies, slots in ((outer_z, [0, 1]), (inner_z, list(range(2, count_z)))):
        for copy in copies:
            copy.wait_recv()
        for slot in slots:
            unrolled(5, 5, lambda part, slot=slot: unpack_z(part, slot))
    sent = moves[0] + moves[1] + moves[2] + x_copies + kind_y
    for copy in sent + outer_copies + inner_copies + outer_z + inner_z:
        copy.wait_send()


def gathered(moved, slots, index, kind):
    extent_x, extent_y, extent_z = kind.shape
    planes = extent_x + 2 * HALO
    peers = lax.axis_size("gy")
    blocks = index.shape[0]
    layers = HALO * moved.shape[2] // extent_x
    vmem = pl.BlockSpec(memory_space=pltpu.VMEM)
    anywhere = pl.BlockSpec(memory_space=pltpu.HBM)
    tile = (SUBLANES, LANES)
    real = jnp.float32
    return pl.pallas_call(
        gather_kernel,
        out_shape=jax.ShapeDtypeStruct((5, planes) + tile, real),
        in_specs=[anywhere] * 4,
        out_specs=vmem,
        scratch_shapes=[
            pltpu.VMEM(moved.shape, real),
            pltpu.SMEM(slots.shape, jnp.int32),
            pltpu.SMEM(index.shape, jnp.int32),
            pltpu.VMEM(kind.shape, jnp.int32),
            pltpu.SemaphoreType.DMA((4,)),
            pltpu.VMEM((peers,) + moved.shape[1:], real),
            pltpu.VMEM((peers, 4, layers), real),
            pltpu.VMEM((peers, 4, layers), real),
            pltpu.VMEM((peers, 4, moved.shape[2] - 2 * layers), real),
            pltpu.VMEM((blocks, 4, layers), real),
            pltpu.VMEM((blocks, 4, layers), real),
            pltpu.VMEM((blocks, 4, moved.shape[2] - 2 * layers), real),
            pltpu.VMEM((2, blocks, 4, layers), real),
            pltpu.VMEM((extent_x, 2) + tile, real),
            pltpu.VMEM((2, HALO) + tile, real),
            pltpu.VMEM((2, extent_x // HALO, 3) + tile, real),
            pltpu.VMEM((2, extent_x // HALO + 2, 3) + tile, real),
            pltpu.VMEM((2, planes // 8, 5) + tile, real),
            pltpu.VMEM((2, planes // 8, 5) + tile, real),
            pltpu.SemaphoreType.DMA((3, peers)),
            pltpu.SemaphoreType.DMA((3, peers)),
            pltpu.SemaphoreType.DMA((24,)),
            pltpu.SemaphoreType.DMA((24,)),
        ],
        compiler_params=pltpu.CompilerParams(
            collective_id=0, has_side_effects=True, vmem_limit_bytes=60 * 1024 * 1024
        ),
        name="gather",
    )(moved, slots, index, kind)


def on_device(moved_fields, send_slot, recv_index, site_kind):
    fields = gathered(
        moved_fields[0, 0, 0],
        send_slot[0, 0, 0].reshape(-1),
        recv_index[0, 0, 0],
        site_kind,
    )
    return lattice(fields, site_kind.shape)


def solution(mesh):
    return jax.shard_map(
        on_device,
        mesh=mesh,
        in_specs=(
            P("gx", "gy", "ba", None, None, None),
            P("gx", "gy", "ba", None, None),
            P("gx", "gy", "ba", None),
            P("gx", "gy", "ba"),
        ),
        out_specs=P(None, "gx", "gy", "ba"),
        check_vma=False,
    )
```

```python
import functools

import jax
import jax.numpy as jnp
from jax import lax
from jax.experimental import pallas as pl
from jax.experimental.pallas import tpu as pltpu
from jax.sharding import PartitionSpec as P

STEPS = 4
HALO = STEPS
PAIRS = (
    (1, 0, 0),
    (0, 1, 0),
    (0, 0, 1),
    (1, 1, 0),
    (1, -1, 0),
    (1, 0, 1),
    (1, 0, -1),
    (0, 1, 1),
    (0, 1, -1),
)
VELOCITIES = ((0, 0, 0),) + tuple(
    tuple(sign * part for part in vector) for vector in PAIRS for sign in (1, -1)
)
WEIGHTS = (1.0 / 3.0,) + (1.0 / 18.0,) * 6 + (1.0 / 36.0,) * 12
RELAX_RATE = 1.25
INLET_SPEED = 0.05
SUBLANES = 8
LANES = 128


def dotted(vector, speeds):
    running = None
    for sign_value, component in zip(vector, speeds):
        if sign_value > 0:
            running = component if running is None else running + component
        elif sign_value < 0:
            running = -component if running is None else running - component
    return running


def row_ids():
    return lax.broadcasted_iota(jnp.int32, (SUBLANES, LANES), 0)


def shifted(plane, rows, stride, step_y, step_z):
    if step_y:
        rolled = pltpu.roll(plane, step_y % SUBLANES, 0)
        crossed = pltpu.roll(rolled, (step_y * stride) % LANES, 1)
        plane = jnp.where(rows == (0 if step_y > 0 else SUBLANES - 1), crossed, rolled)
    if step_z:
        plane = pltpu.roll(plane, step_z % LANES, 1)
    return plane


def unrolled(count, group, body, before=None, after=None):
    def several(sites):
        stores = [entry for site in sites for entry in body(site)]
        for ref, index, value in stores:
            ref[index] = value

    def step(first, carry):
        if before is not None:
            before(first)
        several([first * group + k for k in range(group)])
        if after is not None:
            after(first)
        return carry

    whole = count // group
    if whole > 1:
        lax.fori_loop(0, whole, step, 0)
    elif whole:
        several(range(group))
    if count % group:
        several(range(whole * group, count))


def squared_base(speeds):
    return 1.0 - (1.0 / 6.0) * (
        speeds[0] * speeds[0] + speeds[1] * speeds[1] + speeds[2] * speeds[2]
    )


def start_plane(fields, kind):
    wall, inlet = kind == 1.0, kind == 2.0
    factor = jnp.where(kind <= 1.0, fields[0], 1.0)
    scale = jnp.where(wall, -3.0, jnp.where(inlet, 0.0, 3.0))
    speeds = [scale * fields[axis] for axis in (1, 2, 3)]
    speeds[2] = jnp.where(inlet, 3.0 * INLET_SPEED, speeds[2])
    base = squared_base(speeds)
    result = [WEIGHTS[0] * factor * base]
    weighted = {w: w * factor for w in set(WEIGHTS[1:])}
    for pair_id, vector in enumerate(PAIRS):
        w = weighted[WEIGHTS[1 + 2 * pair_id]]
        projected = dotted(vector, speeds)
        even = w * (base + 0.5 * projected * projected)
        odd = w * projected
        result += [even + odd, even - odd]
    return result


def collide_plane(populations, kind):
    fluid, wall, inlet = kind == 0.0, kind == 1.0, kind == 2.0
    sums = [populations[i] + populations[i + 1] for i in range(1, 19, 2)]
    differences = [populations[i] - populations[i + 1] for i in range(1, 19, 2)]
    density = populations[0]
    for member in sums:
        density = density + member
    triple = 3.0 / density
    speeds = []
    for axis in range(3):
        momentum = dotted([vector[axis] for vector in PAIRS], differences)
        speeds.append(jnp.where(wall | inlet, 0.0, momentum * triple))
    speeds[2] = jnp.where(inlet, 3.0 * INLET_SPEED, speeds[2])
    base = squared_base(speeds)
    factor = jnp.where(fluid, RELAX_RATE * density, jnp.where(wall, 0.0, 1.0))
    keep = jnp.where(fluid, 1.0 - RELAX_RATE, jnp.where(wall, 1.0, 0.0))
    half_even = 0.5 * keep
    half_odd = jnp.where(wall, -0.5, half_even)
    result = [keep * populations[0] + WEIGHTS[0] * factor * base]
    weighted = {w: w * factor for w in set(WEIGHTS[1:])}
    for pair_id, vector in enumerate(PAIRS):
        w = weighted[WEIGHTS[1 + 2 * pair_id]]
        projected = dotted(vector, speeds)
        even = half_even * sums[pair_id] + w * (base + 0.5 * projected * projected)
        odd = half_odd * differences[pair_id] + w * projected
        result += [even + odd, even - odd]
    return result


def lattice_kernel(fields_in, out, fields_ref, result, first, second, in_sem, out_sem):
    planes = fields_ref.shape[1]
    extent_x, extent_y, extent_z = out.shape[1:]

    def load(i):
        cut = pl.ds(2 * i, 2)
        return pltpu.make_async_copy(fields_in.at[:, cut], fields_ref.at[:, cut], in_sem.at[i])

    def save(i):
        cut = pl.ds(2 * i, 2)
        return pltpu.make_async_copy(result.at[:, cut], out.at[:, cut], out_sem.at[i])

    for i in range(planes // 2):
        load(i).start()
    stride = extent_z + 2 * HALO
    rows = row_ids()

    def begin(x):
        fields = [fields_ref[i, x] for i in range(5)]
        return [(first, (i, x), m) for i, m in enumerate(start_plane(fields, fields[4]))]

    unrolled(planes, 2, begin, before=lambda i: load(i).wait())
    source, target = first, second
    for step in range(1, STEPS):

        def advance(x, source=source, target=target, step=step):
            x = x + step
            pulled = [
                shifted(source[i, x - v[0]], rows, stride, v[1], v[2])
                for i, v in enumerate(VELOCITIES)
            ]
            updated = collide_plane(pulled, fields_ref[4, x])
            return [(target, (i, x), member) for i, member in enumerate(updated)]

        unrolled(planes - 2 * step, 2, advance)
        source, target = target, source

    def finish(x):
        stores = []
        for i, v in enumerate(VELOCITIES):
            plane = source[i, x + HALO - v[0]]
            offset = HALO - v[1]
            plane = pltpu.roll(plane, SUBLANES - offset, 0)
            crossed = pltpu.roll(plane, LANES - stride, 1)
            plane = jnp.where(rows < SUBLANES - offset, plane, crossed)
            for group in range(extent_y // SUBLANES):
                part = pltpu.roll(plane, LANES - (group * stride + HALO - v[2]), 1)
                cut = (i, x, pl.ds(group * SUBLANES, SUBLANES), slice(None))
                stores.append((result, cut, part[:, :extent_z]))
        return stores

    unrolled(extent_x, 2, finish, after=lambda i: save(i).start())
    for i in range(extent_x // 2):
        save(i).wait()


def lattice(fields, extents):
    planes = fields.shape[1]
    return pl.pallas_call(
        lattice_kernel,
        out_shape=jax.ShapeDtypeStruct((19,) + tuple(extents), jnp.float32),
        in_specs=[pl.BlockSpec(memory_space=pltpu.HBM)],
        out_specs=pl.BlockSpec(memory_space=pltpu.HBM),
        scratch_shapes=[
            pltpu.VMEM(fields.shape, jnp.float32),
            pltpu.VMEM((19,) + tuple(extents), jnp.float32),
            pltpu.VMEM((19, planes, SUBLANES, LANES), jnp.float32),
            pltpu.VMEM((19, planes, SUBLANES, LANES), jnp.float32),
            pltpu.SemaphoreType.DMA((planes // 2,)),
            pltpu.SemaphoreType.DMA((extents[0] // 2,)),
        ],
        compiler_params=pltpu.CompilerParams(vmem_limit_bytes=60 * 1024 * 1024),
        name="lattice",
    )(fields)


def mesh_device(**moved):
    return tuple(moved.get(axis, lax.axis_index(axis)) for axis in ("gx", "gy", "ba"))


def remote(source, target, send_sem, recv_sem, device):
    return pltpu.make_async_remote_copy(
        src_ref=source,
        dst_ref=target,
        send_sem=send_sem,
        recv_sem=recv_sem,
        device_id=device,
        device_id_type=pl.DeviceIdType.MESH,
    )


def grouped(low, high, rows, lanes, stride):
    middle = pltpu.roll(jnp.where(rows < HALO, low, high), stride, 1)
    last = pltpu.roll(high, 2 * stride, 1)
    return jnp.where(lanes < stride, low, jnp.where(lanes < 2 * stride, middle, last))


def gather_kernel(
    moved_in,
    slot_in,
    index_in,
    kind_in,
    out_ref,
    moved_ref,
    slot_ref,
    index_ref,
    kind_ref,
    input_sem,
    staged,
    arrived_low,
    arrived_high,
    arrived_mid,
    chosen_low,
    chosen_high,
    chosen_mid,
    side_x,
    kind_wide,
    kind_x,
    send_y,
    recv_y,
    send_z,
    side_z,
    sent_sem,
    arrived_sem,
    halo_sent,
    halo_arrived,
):
    inputs = [
        pltpu.make_async_copy(source, target, input_sem.at[i])
        for i, (source, target) in enumerate(
            (
                (slot_in, slot_ref),
                (index_in, index_ref),
                (moved_in, moved_ref),
                (kind_in, kind_ref),
            )
        )
    ]
    for copy in inputs:
        copy.start()
    extent_x, extent_y, extent_z = kind_ref.shape
    blocks = chosen_low.shape[0]
    edge = extent_z // blocks
    stride = extent_z + 2 * HALO
    planes = extent_x + 2 * HALO
    rows = row_ids()
    lanes = lax.broadcasted_iota(jnp.int32, (SUBLANES, LANES), 1)
    me = {axis: lax.axis_index(axis) for axis in ("gx", "gy", "ba")}
    size = {axis: lax.axis_size(axis) for axis in ("gx", "gy", "ba")}
    up = {a: mesh_device(**{a: lax.rem(me[a] + 1, size[a])}) for a in me}
    down = {a: mesh_device(**{a: lax.rem(me[a] + size[a] - 1, size[a])}) for a in me}
    peers = [lax.rem(me["gy"] + offset, size["gy"]) for offset in range(size["gy"])]

    barrier = pltpu.get_barrier_semaphore()
    greeted = [mesh_device(gy=peer) for peer in peers[1:]]
    greeted += [up["gx"], down["gx"], up["ba"], down["ba"]]
    ahead_x, ahead_y = (lax.rem(me[a] + 1, size[a]) for a in ("gx", "gy"))
    behind_x, behind_y = (lax.rem(me[a] + size[a] - 1, size[a]) for a in ("gx", "gy"))
    corners = [
        [mesh_device(gx=x, gy=y) for x in (behind_x, ahead_x)] for y in (behind_y, ahead_y)
    ]
    greeted += corners[0] + corners[1]
    for device in greeted:
        pl.semaphore_signal(
            barrier, inc=1, device_id=device, device_id_type=pl.DeviceIdType.MESH
        )
    for copy in inputs[:3]:
        copy.wait()
    for offset in range(1, size["gy"]):
        staged[offset] = moved_ref[jnp.maximum(slot_ref[peers[offset]], 0)]
    pl.semaphore_wait(barrier, len(greeted))

    plane_size = moved_ref.shape[2] // extent_x
    layers = HALO * plane_size
    pieces = (
        (arrived_low, 0, layers),
        (arrived_high, extent_x * plane_size - layers, layers),
        (arrived_mid, layers, extent_x * plane_size - 2 * layers),
    )
    moves = []
    for number, (target, begin, length) in enumerate(pieces):
        moves.append([])
        for offset in range(1, size["gy"]):
            copy = remote(
                staged.at[offset, :, pl.ds(begin, length)],
                target.at[me["gy"]],
                sent_sem.at[number, offset],
                arrived_sem.at[number, offset],
                mesh_device(gy=peers[offset]),
            )
            copy.start()
            moves[-1].append(copy)
    own_slot = jnp.maximum(slot_ref[me["gy"]], 0)
    for target, begin, length in pieces:
        target[me["gy"]] = moved_ref[own_slot, :, pl.ds(begin, length)]

    def halo(axis, number, low_source, high_source, target):
        pair = [
            remote(
                high_source,
                target.at[0],
                halo_sent.at[2 * number],
                halo_arrived.at[2 * number],
                up[axis],
            ),
            remote(
                low_source,
                target.at[1],
                halo_sent.at[2 * number + 1],
                halo_arrived.at[2 * number + 1],
                down[axis],
            ),
        ]
        for copy in pair:
            copy.start()
        return pair

    quad_lanes = LANES // HALO
    quads = extent_x // HALO

    def pack_y(pair, quad):
        stores = []
        for side in range(2):
            merged = []
            for half in range(2):
                part = min(2 * pair + half, 4)
                total = None
                for k in range(HALO):
                    begin = HALO + (0 if side == 0 else 2 * stride)
                    piece = out_ref[part, quad * HALO + HALO + k]
                    piece = pltpu.roll(piece, (k * quad_lanes - begin) % LANES, 1)
                    total = piece if k == 0 else jnp.where(lanes < k * quad_lanes, total, piece)
                merged.append(total)
            other = pltpu.roll(merged[1], HALO, 0)
            keep = rows >= HALO if side == 0 else rows < HALO
            stores.append((send_y, (side, quad, pair), jnp.where(keep, merged[0], other)))
        return stores

    def unpack_y(pair, quad):
        stores = []
        near, far = recv_y[0, quad, pair], recv_y[1, quad, pair]
        for half in range(1 if pair == 2 else 2):
            part = 2 * pair + half
            if half:
                near, far = pltpu.roll(near, HALO, 0), pltpu.roll(far, HALO, 0)
            for k in range(HALO):
                x = quad * HALO + k
                near_piece = pltpu.roll(near, (HALO - k * quad_lanes) % LANES, 1)
                far_piece = pltpu.roll(
                    far, (HALO + 2 * stride - k * quad_lanes) % LANES, 1
                )
                plane = out_ref[part, x]
                plane = jnp.where((rows < HALO) & (lanes < stride), near_piece, plane)
                plane = jnp.where((rows >= HALO) & (lanes >= 2 * stride), far_piece, plane)
                stores.append((out_ref, (part, x), plane))
        return stores

    last = quads - 1
    outer_y = (
        ("straight", 0, 1, 1),
        ("straight", last, 1, last + 1),
        ("ahead", last, 1, 0),
        ("behind", 0, 1, quads + 1),
    )
    inner_y = (("straight", 1, quads - 2, 2),)
    whole_y = (("straight", 0, quads, 1),) + outer_y[2:]

    def halo_y(first, pairs, routes):
        copies = []
        for toward in range(2):
            devices = {
                "straight": (up if toward else down)["gy"],
                "behind": corners[toward][0],
                "ahead": corners[toward][1],
            }
            for route, source, length, target in routes:
                sem = first + len(copies)
                copies.append(
                    remote(
                        send_y.at[toward, pl.ds(source, length), pairs],
                        recv_y.at[1 - toward, pl.ds(target, length), pairs],
                        halo_sent.at[sem],
                        halo_arrived.at[sem],
                        devices[route],
                    )
                )
                copies[-1].start()
        return copies

    inputs[3].wait()

    def lay_kind(x):
        parts = []
        for half in range(2):
            kind_wide[x, half, :, pl.ds(0, extent_z)] = kind_ref[
                x, pl.ds(half * SUBLANES, SUBLANES), :
            ].astype(jnp.float32)
            wide = pltpu.roll(kind_wide[x, half], HALO, 0)
            parts.append(pltpu.roll(wide, HALO, 1))
        plane = grouped(parts[0], parts[1], rows, lanes, stride)
        return [(out_ref, (4, x + HALO), plane)]

    unrolled(extent_x, 4, lay_kind)
    kind_copies = halo(
        "gx",
        0,
        out_ref.at[4, pl.ds(HALO, HALO)],
        out_ref.at[4, pl.ds(extent_x, HALO)],
        kind_x,
    )
    unrolled(quads, 4, lambda quad: pack_y(2, quad))
    kind_y = halo_y(18, pl.ds(2, 1), whole_y)

    def choose(number, target):
        for copy in moves[number]:
            copy.wait_recv()
        for block in range(blocks):
            target[block] = pieces[number][0][index_ref[block]]

    def lay_fields(read, x, target_x):
        tiles = []
        for block in range(2):
            for half in range(2):
                start = pl.multiple_of(x * plane_size + half * LANES, LANES)
                tiles.append(read(block, pl.ds(start, LANES)))
        quarter, half_lanes, whole = LANES // 4, LANES // 2, LANES
        stores = []
        for part in range(4):
            picked = []
            for source, tile in enumerate(tiles):
                row = jnp.broadcast_to(tile[part : part + 1], (SUBLANES, LANES))
                turned = pltpu.roll(row, half_lanes, 1)
                low_first = (rows >= HALO) == (source % 2 == 0)
                picked.append(jnp.where(low_first, row, turned))
            pairs = []
            for block in range(2):
                pair = jnp.where(lanes < half_lanes, picked[2 * block], picked[2 * block + 1])
                shift = quarter if block else whole - quarter
                turned = pltpu.roll(pair, shift, 1)
                stays = ((rows & 2) == 0) == (block == 0)
                pairs.append(jnp.where(stays, pair, turned))
            joined = jnp.where((lanes & quarter) == 0, pairs[0], pairs[1])
            joined = jnp.where((rows & 1) == 0, joined, pltpu.roll(joined, whole - edge, 1))
            near = pltpu.roll(joined, HALO, 1)
            far = pltpu.roll(joined, (HALO + edge - quarter) % whole, 1)
            low = jnp.where((lanes & (half_lanes - 1)) < HALO + edge, near, far)
            high = pltpu.roll(low, half_lanes, 1)
            plane = grouped(low, high, rows, lanes, stride)
            stores.append((out_ref, (part, target_x), plane))
        return stores

    def lay_own(source, count, first_x):
        def lay(x):
            return lay_fields(lambda block, cut: source[block, :, cut], x, first_x + x)

        unrolled(count, 2, lay)

    choose(0, chosen_low)
    choose(1, chosen_high)
    x_copies = halo("gx", 1, chosen_low, chosen_high, side_x)
    lay_own(chosen_low, HALO, HALO)
    lay_own(chosen_high, HALO, extent_x)
    for pair in range(2):
        unrolled(2, 2, lambda k, pair=pair: pack_y(pair, k * last))
    outer_copies = halo_y(8, pl.ds(0, 2), outer_y)
    for copy in kind_copies:
        copy.wait()
    for copy in x_copies:
        copy.wait_recv()

    for side in range(2):
        first_x = side * (extent_x + HALO)

        def lay_side(x, side=side, first_x=first_x):
            stores = lay_fields(
                lambda block, cut: side_x[side, block, :, cut], x, first_x + x
            )
            return stores + [(out_ref, (4, first_x + x), kind_x[side, x])]

        unrolled(HALO, 2, lay_side)

    choose(2, chosen_mid)
    lay_own(chosen_mid, extent_x - 2 * HALO, 2 * HALO)
    for pair in range(2):
        unrolled(quads - 2, 2, lambda k, pair=pair: pack_y(pair, 1 + k))
    inner_copies = halo_y(16, pl.ds(0, 2), inner_y)

    per_z = 8
    count_z = planes // per_z
    column = lax.rem(lanes, stride)

    def pack_z(part, slot):
        stores = []
        first_x = group_z[slot] * per_z
        own = [out_ref[part, first_x + k] for k in range(per_z)]
        for side in range(2):
            begin = HALO if side == 0 else extent_z
            total = None
            for k in range(per_z):
                shift = (k * HALO - begin) % LANES
                piece = pltpu.roll(own[k], shift, 1) if shift else own[k]
                total = piece if k == 0 else jnp.where(column < k * HALO, total, piece)
            stores.append((send_z, (side, slot, part), total))
        return stores

    def unpack_z(part, slot):
        stores = []
        first_x = group_z[slot] * per_z
        near, far = side_z[0, slot, part], side_z[1, slot, part]
        for k in range(per_z):
            back = (-k * HALO) % LANES
            ahead = (HALO + extent_z - k * HALO) % LANES
            near_piece = pltpu.roll(near, back, 1) if back else near
            far_piece = pltpu.roll(far, ahead, 1) if ahead else far
            plane = out_ref[part, first_x + k]
            plane = jnp.where(column < HALO, near_piece, plane)
            plane = jnp.where(column >= HALO + extent_z, far_piece, plane)
            stores.append((out_ref, (part, first_x + k), plane))
        return stores

    def exchange_z(number, slots):
        for slot in slots:
            unrolled(5, 5, lambda part, slot=slot: pack_z(part, slot))
        cut = pl.ds(slots[0], len(slots))
        return halo("ba", number, send_z.at[0, cut], send_z.at[1, cut], side_z.at[:, cut])

    group_z = [0] + [count_z - 1] + list(range(1, count_z - 1))
    for copy in outer_copies + kind_y:
        copy.wait_recv()
    for pair in range(3):
        unrolled(2, 2, lambda k, pair=pair: unpack_y(pair, k))
        unrolled(2, 2, lambda k, pair=pair: unpack_y(pair, quads + k))
    outer_z = exchange_z(2, [0, 1])
    for copy in inner_copies:
        copy.wait_recv()
    for pair in range(3):
        unrolled(2, 2, lambda k, pair=pair: unpack_y(pair, 2 + k))
    inner_z = exchange_z(3, list(range(2, count_z)))
    for copies, slots in ((outer_z, [0, 1]), (inner_z, list(range(2, count_z)))):
        for copy in copies:
            copy.wait_recv()
        for slot in slots:
            unrolled(5, 5, lambda part, slot=slot: unpack_z(part, slot))
    sent = moves[0] + moves[1] + moves[2] + x_copies + kind_y
    for copy in sent + outer_copies + inner_copies + outer_z + inner_z:
        copy.wait_send()


def gathered(moved, slots, index, kind):
    extent_x, extent_y, extent_z = kind.shape
    planes = extent_x + 2 * HALO
    peers = lax.axis_size("gy")
    blocks = index.shape[0]
    layers = HALO * moved.shape[2] // extent_x
    vmem = pl.BlockSpec(memory_space=pltpu.VMEM)
    anywhere = pl.BlockSpec(memory_space=pltpu.HBM)
    tile = (SUBLANES, LANES)
    real = jnp.float32
    return pl.pallas_call(
        gather_kernel,
        out_shape=jax.ShapeDtypeStruct((5, planes) + tile, real),
        in_specs=[anywhere] * 4,
        out_specs=vmem,
        scratch_shapes=[
            pltpu.VMEM(moved.shape, real),
            pltpu.SMEM(slots.shape, jnp.int32),
            pltpu.SMEM(index.shape, jnp.int32),
            pltpu.VMEM(kind.shape, jnp.int32),
            pltpu.SemaphoreType.DMA((4,)),
            pltpu.VMEM((peers,) + moved.shape[1:], real),
            pltpu.VMEM((peers, 4, layers), real),
            pltpu.VMEM((peers, 4, layers), real),
            pltpu.VMEM((peers, 4, moved.shape[2] - 2 * layers), real),
            pltpu.VMEM((blocks, 4, layers), real),
            pltpu.VMEM((blocks, 4, layers), real),
            pltpu.VMEM((blocks, 4, moved.shape[2] - 2 * layers), real),
            pltpu.VMEM((2, blocks, 4, layers), real),
            pltpu.VMEM((extent_x, 2) + tile, real),
            pltpu.VMEM((2, HALO) + tile, real),
            pltpu.VMEM((2, extent_x // HALO, 3) + tile, real),
            pltpu.VMEM((2, extent_x // HALO + 2, 3) + tile, real),
            pltpu.VMEM((2, planes // 8, 5) + tile, real),
            pltpu.VMEM((2, planes // 8, 5) + tile, real),
            pltpu.SemaphoreType.DMA((3, peers)),
            pltpu.SemaphoreType.DMA((3, peers)),
            pltpu.SemaphoreType.DMA((24,)),
            pltpu.SemaphoreType.DMA((24,)),
        ],
        compiler_params=pltpu.CompilerParams(
            collective_id=0, has_side_effects=True, vmem_limit_bytes=60 * 1024 * 1024
        ),
        name="gather",
    )(moved, slots, index, kind)


def on_device(moved_fields, send_slot, recv_index, site_kind):
    fields = gathered(
        moved_fields[0, 0, 0],
        send_slot[0, 0, 0].reshape(-1),
        recv_index[0, 0, 0],
        site_kind,
    )
    return lattice(fields, site_kind.shape)


def solution(mesh):
    return jax.shard_map(
        on_device,
        mesh=mesh,
        in_specs=(
            P("gx", "gy", "ba", None, None, None),
            P("gx", "gy", "ba", None, None),
            P("gx", "gy", "ba", None),
            P("gx", "gy", "ba"),
        ),
        out_specs=P(None, "gx", "gy", "ba"),
        check_vma=False,
    )
```

```python
import functools

import jax
import jax.numpy as jnp
from jax import lax
from jax.experimental import pallas as pl
from jax.experimental.pallas import tpu as pltpu
from jax.sharding import PartitionSpec as P

STEPS = 4
HALO = STEPS
PAIRS = (
    (1, 0, 0),
    (0, 1, 0),
    (0, 0, 1),
    (1, 1, 0),
    (1, -1, 0),
    (1, 0, 1),
    (1, 0, -1),
    (0, 1, 1),
    (0, 1, -1),
)
VELOCITIES = ((0, 0, 0),) + tuple(
    tuple(sign * part for part in vector) for vector in PAIRS for sign in (1, -1)
)
WEIGHTS = (1.0 / 3.0,) + (1.0 / 18.0,) * 6 + (1.0 / 36.0,) * 12
RELAX_RATE = 1.25
INLET_SPEED = 0.05
SUBLANES = 8
LANES = 128


def dotted(vector, speeds):
    running = None
    for sign_value, component in zip(vector, speeds):
        if sign_value > 0:
            running = component if running is None else running + component
        elif sign_value < 0:
            running = -component if running is None else running - component
    return running


def row_ids():
    return lax.broadcasted_iota(jnp.int32, (SUBLANES, LANES), 0)


def shifted(plane, rows, stride, step_y, step_z):
    if step_y:
        rolled = pltpu.roll(plane, step_y % SUBLANES, 0)
        crossed = pltpu.roll(rolled, (step_y * stride) % LANES, 1)
        plane = jnp.where(rows == (0 if step_y > 0 else SUBLANES - 1), crossed, rolled)
    if step_z:
        plane = pltpu.roll(plane, step_z % LANES, 1)
    return plane


def unrolled(count, group, body, before=None, after=None):
    def several(sites):
        stores = [entry for site in sites for entry in body(site)]
        for ref, index, value in stores:
            ref[index] = value

    def step(first, carry):
        if before is not None:
            before(first)
        several([first * group + k for k in range(group)])
        if after is not None:
            after(first)
        return carry

    whole = count // group
    if whole > 1:
        lax.fori_loop(0, whole, step, 0)
    elif whole:
        several(range(group))
    if count % group:
        several(range(whole * group, count))


def squared_base(speeds):
    return 1.0 - (1.0 / 6.0) * (
        speeds[0] * speeds[0] + speeds[1] * speeds[1] + speeds[2] * speeds[2]
    )


def start_plane(fields, kind):
    wall, inlet = kind == 1.0, kind == 2.0
    factor = jnp.where(kind <= 1.0, fields[0], 1.0)
    scale = jnp.where(wall, -3.0, jnp.where(inlet, 0.0, 3.0))
    speeds = [scale * fields[axis] for axis in (1, 2, 3)]
    speeds[2] = jnp.where(inlet, 3.0 * INLET_SPEED, speeds[2])
    base = squared_base(speeds)
    result = [WEIGHTS[0] * factor * base]
    weighted = {w: w * factor for w in set(WEIGHTS[1:])}
    for pair_id, vector in enumerate(PAIRS):
        w = weighted[WEIGHTS[1 + 2 * pair_id]]
        projected = dotted(vector, speeds)
        even = w * (base + 0.5 * projected * projected)
        odd = w * projected
        result += [even + odd, even - odd]
    return result


def collide_plane(populations, kind):
    fluid, wall, inlet = kind == 0.0, kind == 1.0, kind == 2.0
    sums = [populations[i] + populations[i + 1] for i in range(1, 19, 2)]
    differences = [populations[i] - populations[i + 1] for i in range(1, 19, 2)]
    density = populations[0]
    for member in sums:
        density = density + member
    triple = 3.0 / density
    speeds = []
    for axis in range(3):
        momentum = dotted([vector[axis] for vector in PAIRS], differences)
        speeds.append(jnp.where(wall | inlet, 0.0, momentum * triple))
    speeds[2] = jnp.where(inlet, 3.0 * INLET_SPEED, speeds[2])
    base = squared_base(speeds)
    factor = jnp.where(fluid, RELAX_RATE * density, jnp.where(wall, 0.0, 1.0))
    keep = jnp.where(fluid, 1.0 - RELAX_RATE, jnp.where(wall, 1.0, 0.0))
    half_even = 0.5 * keep
    half_odd = jnp.where(wall, -0.5, half_even)
    result = [keep * populations[0] + WEIGHTS[0] * factor * base]
    weighted = {w: w * factor for w in set(WEIGHTS[1:])}
    for pair_id, vector in enumerate(PAIRS):
        w = weighted[WEIGHTS[1 + 2 * pair_id]]
        projected = dotted(vector, speeds)
        even = half_even * sums[pair_id] + w * (base + 0.5 * projected * projected)
        odd = half_odd * differences[pair_id] + w * projected
        result += [even + odd, even - odd]
    return result


def lattice_kernel(fields_in, out, fields_ref, result, first, second, in_sem, out_sem):
    planes = fields_ref.shape[1]
    extent_x, extent_y, extent_z = out.shape[1:]

    def load(i):
        cut = pl.ds(2 * i, 2)
        return pltpu.make_async_copy(fields_in.at[:, cut], fields_ref.at[:, cut], in_sem.at[i])

    def save(i):
        cut = pl.ds(2 * i, 2)
        return pltpu.make_async_copy(result.at[:, cut], out.at[:, cut], out_sem.at[i])

    for i in range(planes // 2):
        load(i).start()
    stride = extent_z + 2 * HALO
    rows = row_ids()

    def begin(x):
        fields = [fields_ref[i, x] for i in range(5)]
        return [(first, (i, x), m) for i, m in enumerate(start_plane(fields, fields[4]))]

    unrolled(planes, 2, begin, before=lambda i: load(i).wait())
    source, target = first, second
    for step in range(1, STEPS):

        def advance(x, source=source, target=target, step=step):
            x = x + step
            pulled = [
                shifted(source[i, x - v[0]], rows, stride, v[1], v[2])
                for i, v in enumerate(VELOCITIES)
            ]
            updated = collide_plane(pulled, fields_ref[4, x])
            return [(target, (i, x), member) for i, member in enumerate(updated)]

        unrolled(planes - 2 * step, 2, advance)
        source, target = target, source

    def finish(x):
        stores = []
        for i, v in enumerate(VELOCITIES):
            plane = source[i, x + HALO - v[0]]
            offset = HALO - v[1]
            plane = pltpu.roll(plane, SUBLANES - offset, 0)
            crossed = pltpu.roll(plane, LANES - stride, 1)
            plane = jnp.where(rows < SUBLANES - offset, plane, crossed)
            for group in range(extent_y // SUBLANES):
                part = pltpu.roll(plane, LANES - (group * stride + HALO - v[2]), 1)
                cut = (i, x, pl.ds(group * SUBLANES, SUBLANES), slice(None))
                stores.append((result, cut, part[:, :extent_z]))
        return stores

    unrolled(extent_x, 2, finish, after=lambda i: save(i).start())
    for i in range(extent_x // 2):
        save(i).wait()


def lattice(fields, extents):
    planes = fields.shape[1]
    return pl.pallas_call(
        lattice_kernel,
        out_shape=jax.ShapeDtypeStruct((19,) + tuple(extents), jnp.float32),
        in_specs=[pl.BlockSpec(memory_space=pltpu.HBM)],
        out_specs=pl.BlockSpec(memory_space=pltpu.HBM),
        scratch_shapes=[
            pltpu.VMEM(fields.shape, jnp.float32),
            pltpu.VMEM((19,) + tuple(extents), jnp.float32),
            pltpu.VMEM((19, planes, SUBLANES, LANES), jnp.float32),
            pltpu.VMEM((19, planes, SUBLANES, LANES), jnp.float32),
            pltpu.SemaphoreType.DMA((planes // 2,)),
            pltpu.SemaphoreType.DMA((extents[0] // 2,)),
        ],
        compiler_params=pltpu.CompilerParams(vmem_limit_bytes=60 * 1024 * 1024),
        name="lattice",
    )(fields)


def mesh_device(**moved):
    return tuple(moved.get(axis, lax.axis_index(axis)) for axis in ("gx", "gy", "ba"))


def remote(source, target, send_sem, recv_sem, device):
    return pltpu.make_async_remote_copy(
        src_ref=source,
        dst_ref=target,
        send_sem=send_sem,
        recv_sem=recv_sem,
        device_id=device,
        device_id_type=pl.DeviceIdType.MESH,
    )


def grouped(low, high, rows, lanes, stride):
    middle = pltpu.roll(jnp.where(rows < HALO, low, high), stride, 1)
    last = pltpu.roll(high, 2 * stride, 1)
    return jnp.where(lanes < stride, low, jnp.where(lanes < 2 * stride, middle, last))


def gather_kernel(
    moved_in,
    slot_in,
    index_in,
    kind_in,
    out_ref,
    moved_ref,
    slot_ref,
    index_ref,
    kind_ref,
    input_sem,
    staged,
    arrived_low,
    arrived_high,
    arrived_mid,
    chosen_low,
    chosen_high,
    chosen_mid,
    side_x,
    kind_wide,
    kind_x,
    send_y,
    recv_y,
    send_z,
    side_z,
    sent_sem,
    arrived_sem,
    halo_sent,
    halo_arrived,
):
    inputs = [
        pltpu.make_async_copy(source, target, input_sem.at[i])
        for i, (source, target) in enumerate(
            (
                (slot_in, slot_ref),
                (index_in, index_ref),
                (moved_in, moved_ref),
                (kind_in, kind_ref),
            )
        )
    ]
    for copy in inputs:
        copy.start()
    extent_x, extent_y, extent_z = kind_ref.shape
    blocks = chosen_low.shape[0]
    edge = extent_z // blocks
    stride = extent_z + 2 * HALO
    planes = extent_x + 2 * HALO
    rows = row_ids()
    lanes = lax.broadcasted_iota(jnp.int32, (SUBLANES, LANES), 1)
    me = {axis: lax.axis_index(axis) for axis in ("gx", "gy", "ba")}
    size = {axis: lax.axis_size(axis) for axis in ("gx", "gy", "ba")}
    up = {a: mesh_device(**{a: lax.rem(me[a] + 1, size[a])}) for a in me}
    down = {a: mesh_device(**{a: lax.rem(me[a] + size[a] - 1, size[a])}) for a in me}
    peers = [lax.rem(me["gy"] + offset, size["gy"]) for offset in range(size["gy"])]

    barrier = pltpu.get_barrier_semaphore()
    greeted = [mesh_device(gy=peer) for peer in peers[1:]]
    greeted += [up["gx"], down["gx"], up["ba"], down["ba"]]
    ahead_x, ahead_y = (lax.rem(me[a] + 1, size[a]) for a in ("gx", "gy"))
    behind_x, behind_y = (lax.rem(me[a] + size[a] - 1, size[a]) for a in ("gx", "gy"))
    corners = [
        [mesh_device(gx=x, gy=y) for x in (behind_x, ahead_x)] for y in (behind_y, ahead_y)
    ]
    greeted += corners[0] + corners[1]
    for device in greeted:
        pl.semaphore_signal(
            barrier, inc=1, device_id=device, device_id_type=pl.DeviceIdType.MESH
        )
    for copy in inputs[:3]:
        copy.wait()
    for offset in range(1, size["gy"]):
        staged[offset] = moved_ref[jnp.maximum(slot_ref[peers[offset]], 0)]
    pl.semaphore_wait(barrier, len(greeted))

    plane_size = moved_ref.shape[2] // extent_x
    layers = HALO * plane_size
    pieces = (
        (arrived_low, 0, layers),
        (arrived_high, extent_x * plane_size - layers, layers),
        (arrived_mid, layers, extent_x * plane_size - 2 * layers),
    )
    moves = []
    for number, (target, begin, length) in enumerate(pieces):
        moves.append([])
        for offset in range(1, size["gy"]):
            copy = remote(
                staged.at[offset, :, pl.ds(begin, length)],
                target.at[me["gy"]],
                sent_sem.at[number, offset],
                arrived_sem.at[number, offset],
                mesh_device(gy=peers[offset]),
            )
            copy.start()
            moves[-1].append(copy)
    own_slot = jnp.maximum(slot_ref[me["gy"]], 0)
    for target, begin, length in pieces:
        target[me["gy"]] = moved_ref[own_slot, :, pl.ds(begin, length)]

    def halo(axis, number, low_source, high_source, target):
        pair = [
            remote(
                high_source,
                target.at[0],
                halo_sent.at[2 * number],
                halo_arrived.at[2 * number],
                up[axis],
            ),
            remote(
                low_source,
                target.at[1],
                halo_sent.at[2 * number + 1],
                halo_arrived.at[2 * number + 1],
                down[axis],
            ),
        ]
        for copy in pair:
            copy.start()
        return pair

    quad_lanes = LANES // HALO
    quads = extent_x // HALO

    def pack_y(pair, quad):
        stores = []
        for side in range(2):
            merged = []
            for half in range(2):
                part = min(2 * pair + half, 4)
                total = None
                for k in range(HALO):
                    begin = HALO + (0 if side == 0 else 2 * stride)
                    piece = out_ref[part, quad * HALO + HALO + k]
                    piece = pltpu.roll(piece, (k * quad_lanes - begin) % LANES, 1)
                    total = piece if k == 0 else jnp.where(lanes < k * quad_lanes, total, piece)
                merged.append(total)
            other = pltpu.roll(merged[1], HALO, 0)
            keep = rows >= HALO if side == 0 else rows < HALO
            stores.append((send_y, (side, quad, pair), jnp.where(keep, merged[0], other)))
        return stores

    def unpack_y(pair, quad):
        stores = []
        near, far = recv_y[0, quad, pair], recv_y[1, quad, pair]
        for half in range(1 if pair == 2 else 2):
            part = 2 * pair + half
            if half:
                near, far = pltpu.roll(near, HALO, 0), pltpu.roll(far, HALO, 0)
            for k in range(HALO):
                x = quad * HALO + k
                near_piece = pltpu.roll(near, (HALO - k * quad_lanes) % LANES, 1)
                far_piece = pltpu.roll(
                    far, (HALO + 2 * stride - k * quad_lanes) % LANES, 1
                )
                plane = out_ref[part, x]
                plane = jnp.where((rows < HALO) & (lanes < stride), near_piece, plane)
                plane = jnp.where((rows >= HALO) & (lanes >= 2 * stride), far_piece, plane)
                stores.append((out_ref, (part, x), plane))
        return stores

    last = quads - 1
    outer_y = (
        ("straight", 0, 1, 1),
        ("straight", last, 1, last + 1),
        ("ahead", last, 1, 0),
        ("behind", 0, 1, quads + 1),
    )
    inner_y = (("straight", 1, quads - 2, 2),)
    whole_y = (("straight", 0, quads, 1),) + outer_y[2:]

    def halo_y(first, pairs, routes):
        copies = []
        for toward in range(2):
            devices = {
                "straight": (up if toward else down)["gy"],
                "behind": corners[toward][0],
                "ahead": corners[toward][1],
            }
            for route, source, length, target in routes:
                sem = first + len(copies)
                copies.append(
                    remote(
                        send_y.at[toward, pl.ds(source, length), pairs],
                        recv_y.at[1 - toward, pl.ds(target, length), pairs],
                        halo_sent.at[sem],
                        halo_arrived.at[sem],
                        devices[route],
                    )
                )
                copies[-1].start()
        return copies

    inputs[3].wait()

    def lay_kind(x):
        parts = []
        for half in range(2):
            kind_wide[x, half, :, pl.ds(0, extent_z)] = kind_ref[
                x, pl.ds(half * SUBLANES, SUBLANES), :
            ].astype(jnp.float32)
            wide = pltpu.roll(kind_wide[x, half], HALO, 0)
            parts.append(pltpu.roll(wide, HALO, 1))
        plane = grouped(parts[0], parts[1], rows, lanes, stride)
        return [(out_ref, (4, x + HALO), plane)]

    unrolled(extent_x, 8, lay_kind)
    kind_copies = halo(
        "gx",
        0,
        out_ref.at[4, pl.ds(HALO, HALO)],
        out_ref.at[4, pl.ds(extent_x, HALO)],
        kind_x,
    )
    unrolled(quads, 4, lambda quad: pack_y(2, quad))
    kind_y = halo_y(18, pl.ds(2, 1), whole_y)

    def choose(number, target):
        for copy in moves[number]:
            copy.wait_recv()
        for block in range(blocks):
            target[block] = pieces[number][0][index_ref[block]]

    def lay_fields(read, x, target_x):
        tiles = []
        for block in range(2):
            for half in range(2):
                start = pl.multiple_of(x * plane_size + half * LANES, LANES)
                tiles.append(read(block, pl.ds(start, LANES)))
        quarter, half_lanes, whole = LANES // 4, LANES // 2, LANES
        stores = []
        for part in range(4):
            picked = []
            for source, tile in enumerate(tiles):
                row = jnp.broadcast_to(tile[part : part + 1], (SUBLANES, LANES))
                turned = pltpu.roll(row, half_lanes, 1)
                low_first = (rows >= HALO) == (source % 2 == 0)
                picked.append(jnp.where(low_first, row, turned))
            pairs = []
            for block in range(2):
                pair = jnp.where(lanes < half_lanes, picked[2 * block], picked[2 * block + 1])
                shift = quarter if block else whole - quarter
                turned = pltpu.roll(pair, shift, 1)
                stays = ((rows & 2) == 0) == (block == 0)
                pairs.append(jnp.where(stays, pair, turned))
            joined = jnp.where((lanes & quarter) == 0, pairs[0], pairs[1])
            joined = jnp.where((rows & 1) == 0, joined, pltpu.roll(joined, whole - edge, 1))
            near = pltpu.roll(joined, HALO, 1)
            far = pltpu.roll(joined, (HALO + edge - quarter) % whole, 1)
            low = jnp.where((lanes & (half_lanes - 1)) < HALO + edge, near, far)
            high = pltpu.roll(low, half_lanes, 1)
            plane = grouped(low, high, rows, lanes, stride)
            stores.append((out_ref, (part, target_x), plane))
        return stores

    def lay_own(source, count, first_x):
        def lay(x):
            return lay_fields(lambda block, cut: source[block, :, cut], x, first_x + x)

        unrolled(count, 8, lay)

    choose(0, chosen_low)
    choose(1, chosen_high)
    x_copies = halo("gx", 1, chosen_low, chosen_high, side_x)
    lay_own(chosen_low, HALO, HALO)
    lay_own(chosen_high, HALO, extent_x)
    for pair in range(2):
        unrolled(2, 2, lambda k, pair=pair: pack_y(pair, k * last))
    outer_copies = halo_y(8, pl.ds(0, 2), outer_y)
    for copy in kind_copies:
        copy.wait()
    for copy in x_copies:
        copy.wait_recv()

    for side in range(2):
        first_x = side * (extent_x + HALO)

        def lay_side(x, side=side, first_x=first_x):
            stores = lay_fields(
                lambda block, cut: side_x[side, block, :, cut], x, first_x + x
            )
            return stores + [(out_ref, (4, first_x + x), kind_x[side, x])]

        unrolled(HALO, 4, lay_side)

    choose(2, chosen_mid)
    lay_own(chosen_mid, extent_x - 2 * HALO, 2 * HALO)
    for pair in range(2):
        unrolled(quads - 2, 2, lambda k, pair=pair: pack_y(pair, 1 + k))
    inner_copies = halo_y(16, pl.ds(0, 2), inner_y)

    per_z = 8
    count_z = planes // per_z
    column = lax.rem(lanes, stride)

    def pack_z(part, slot):
        stores = []
        first_x = group_z[slot] * per_z
        own = [out_ref[part, first_x + k] for k in range(per_z)]
        for side in range(2):
            begin = HALO if side == 0 else extent_z
            total = None
            for k in range(per_z):
                shift = (k * HALO - begin) % LANES
                piece = pltpu.roll(own[k], shift, 1) if shift else own[k]
                total = piece if k == 0 else jnp.where(column < k * HALO, total, piece)
            stores.append((send_z, (side, slot, part), total))
        return stores

    def unpack_z(part, slot):
        stores = []
        first_x = group_z[slot] * per_z
        near, far = side_z[0, slot, part], side_z[1, slot, part]
        for k in range(per_z):
            back = (-k * HALO) % LANES
            ahead = (HALO + extent_z - k * HALO) % LANES
            near_piece = pltpu.roll(near, back, 1) if back else near
            far_piece = pltpu.roll(far, ahead, 1) if ahead else far
            plane = out_ref[part, first_x + k]
            plane = jnp.where(column < HALO, near_piece, plane)
            plane = jnp.where(column >= HALO + extent_z, far_piece, plane)
            stores.append((out_ref, (part, first_x + k), plane))
        return stores

    def exchange_z(number, slots):
        for slot in slots:
            unrolled(5, 5, lambda part, slot=slot: pack_z(part, slot))
        cut = pl.ds(slots[0], len(slots))
        return halo("ba", number, send_z.at[0, cut], send_z.at[1, cut], side_z.at[:, cut])

    group_z = [0] + [count_z - 1] + list(range(1, count_z - 1))
    for copy in outer_copies + kind_y:
        copy.wait_recv()
    for pair in range(3):
        unrolled(2, 2, lambda k, pair=pair: unpack_y(pair, k))
        unrolled(2, 2, lambda k, pair=pair: unpack_y(pair, quads + k))
    outer_z = exchange_z(2, [0, 1])
    for copy in inner_copies:
        copy.wait_recv()
    for pair in range(3):
        unrolled(2, 2, lambda k, pair=pair: unpack_y(pair, 2 + k))
    inner_z = exchange_z(3, list(range(2, count_z)))
    for copies, slots in ((outer_z, [0, 1]), (inner_z, list(range(2, count_z)))):
        for copy in copies:
            copy.wait_recv()
        for slot in slots:
            unrolled(5, 5, lambda part, slot=slot: unpack_z(part, slot))
    sent = moves[0] + moves[1] + moves[2] + x_copies + kind_y
    for copy in sent + outer_copies + inner_copies + outer_z + inner_z:
        copy.wait_send()


def gathered(moved, slots, index, kind):
    extent_x, extent_y, extent_z = kind.shape
    planes = extent_x + 2 * HALO
    peers = lax.axis_size("gy")
    blocks = index.shape[0]
    layers = HALO * moved.shape[2] // extent_x
    vmem = pl.BlockSpec(memory_space=pltpu.VMEM)
    anywhere = pl.BlockSpec(memory_space=pltpu.HBM)
    tile = (SUBLANES, LANES)
    real = jnp.float32
    return pl.pallas_call(
        gather_kernel,
        out_shape=jax.ShapeDtypeStruct((5, planes) + tile, real),
        in_specs=[anywhere] * 4,
        out_specs=vmem,
        scratch_shapes=[
            pltpu.VMEM(moved.shape, real),
            pltpu.SMEM(slots.shape, jnp.int32),
            pltpu.SMEM(index.shape, jnp.int32),
            pltpu.VMEM(kind.shape, jnp.int32),
            pltpu.SemaphoreType.DMA((4,)),
            pltpu.VMEM((peers,) + moved.shape[1:], real),
            pltpu.VMEM((peers, 4, layers), real),
            pltpu.VMEM((peers, 4, layers), real),
            pltpu.VMEM((peers, 4, moved.shape[2] - 2 * layers), real),
            pltpu.VMEM((blocks, 4, layers), real),
            pltpu.VMEM((blocks, 4, layers), real),
            pltpu.VMEM((blocks, 4, moved.shape[2] - 2 * layers), real),
            pltpu.VMEM((2, blocks, 4, layers), real),
            pltpu.VMEM((extent_x, 2) + tile, real),
            pltpu.VMEM((2, HALO) + tile, real),
            pltpu.VMEM((2, extent_x // HALO, 3) + tile, real),
            pltpu.VMEM((2, extent_x // HALO + 2, 3) + tile, real),
            pltpu.VMEM((2, planes // 8, 5) + tile, real),
            pltpu.VMEM((2, planes // 8, 5) + tile, real),
            pltpu.SemaphoreType.DMA((3, peers)),
            pltpu.SemaphoreType.DMA((3, peers)),
            pltpu.SemaphoreType.DMA((24,)),
            pltpu.SemaphoreType.DMA((24,)),
        ],
        compiler_params=pltpu.CompilerParams(
            collective_id=0, has_side_effects=True, vmem_limit_bytes=60 * 1024 * 1024
        ),
        name="gather",
    )(moved, slots, index, kind)


def on_device(moved_fields, send_slot, recv_index, site_kind):
    fields = gathered(
        moved_fields[0, 0, 0],
        send_slot[0, 0, 0].reshape(-1),
        recv_index[0, 0, 0],
        site_kind,
    )
    return lattice(fields, site_kind.shape)


def solution(mesh):
    return jax.shard_map(
        on_device,
        mesh=mesh,
        in_specs=(
            P("gx", "gy", "ba", None, None, None),
            P("gx", "gy", "ba", None, None),
            P("gx", "gy", "ba", None),
            P("gx", "gy", "ba"),
        ),
        out_specs=P(None, "gx", "gy", "ba"),
        check_vma=False,
    )
```
